32 devices in a mesh: frames: 8 (over y, x, core), chan: 4 (over z).
Axes of the slice: x: 2, y: 2, z: 4, core: 2. Of those that a mesh axis runs over, the one named last changes fastest.
Arguments:
- fields: bfloat16 [8, 3, 72, 64, 1536], P('frames', None, 'chan'), may hold values from -6 to 6
- lead_index: int32 [8], P('frames'), may hold values from 0 to 39
- embed_weight: bfloat16 [3, 72, 64, 768], P(None, 'chan'), may hold values from -0.0546875 to 0.0546875
- position_embed: bfloat16 [1536, 768], P('chan'), may hold values from -3 to 3
- lead_table: bfloat16 [40, 768], replicated, may hold values from -3 to 3
- attend_gain: float32 [768], replicated, may hold values from 0.5 to 1.5
- attend_shift: float32 [768], replicated, may hold values from -1.2 to 1.2
- attend_weight: bfloat16 [768, 2304], replicated, may hold values from -0.21875 to 0.21875
- out_weight: bfloat16 [768, 768], replicated, may hold values from -0.875 to 0.875
- out_bias: float32 [768], replicated, may hold values from -1.2 to 1.2
- mixer_gain: float32 [768], replicated, may hold values from 0.5 to 1.5
- mixer_shift: float32 [768], replicated, may hold values from -1.2 to 1.2
- up_weight: bfloat16 [768, 3072], replicated, may hold values from -0.21875 to 0.21875
- up_bias: float32 [3072], replicated, may hold values from -1.2 to 1.2
- down_weight: bfloat16 [3072, 768], replicated, may hold values from -0.109375 to 0.109375
- down_bias: float32 [768], replicated, may hold values from -1.2 to 1.2
- head_weight: bfloat16 [768, 192], replicated, may hold values from -0.109375 to 0.109375
- specialist_cell_offset: float32 [3, 72, 64], P(None, 'chan'), may hold values from -3 to 3
- cotangent: bfloat16 [8, 72, 64, 1536], P('frames', 'chan'), may hold values from -6 to 6
Outputs:
- mixed_prediction: bfloat16 [8, 72, 64, 1536], P('frames', 'chan')
- fields_grad: bfloat16 [8, 3, 72, 64, 1536], P('frames', None, 'chan')
- embed_grad: float32 [3, 72, 64, 768], P(None, 'chan', None, 'frames')
- position_grad: float32 [1536, 768], P('chan', 'frames')
- table_grad: float32 [40, 768], P(None, ('frames', 'chan'))
- attend_gain_grad: float32 [768], P(('frames', 'chan'))
- attend_shift_grad: float32 [768], P(('frames', 'chan'))
- attend_weight_grad: float32 [768, 2304], P(('frames', 'chan'))
- out_weight_grad: float32 [768, 768], P(('frames', 'chan'))
- out_bias_grad: float32 [768], P(('frames', 'chan'))
- mixer_gain_grad: float32 [768], P(('frames', 'chan'))
- mixer_shift_grad: float32 [768], P(('frames', 'chan'))
- up_weight_grad: float32 [768, 3072], P(('frames', 'chan'))
- up_bias_grad: float32 [3072], P(('frames', 'chan'))
- down_weight_grad: float32 [3072, 768], P(('frames', 'chan'))
- down_bias_grad: float32 [768], P(('frames', 'chan'))
- head_weight_grad: float32 [768, 192], P(('frames', 'chan'))
- expert_bias_grad: float32 [3, 72, 64], P(None, 'chan', 'frames')
The draws below stay inside these ranges and needn't reach their ends.
All inputs are finite; a program needn't handle non-finite values.
Results may differ from the reference program's by a relative error of at most 0.023.
Values may be sent and summed in bfloat16 or wider, within the bound.
No kernel may reach another device: no remote copies, remote signals or barrier semaphores. Data moves between devices by JAX's collectives and lax.ppermute only.
A program may use at most 320 MiB of HBM per device.

```python
import math
import jax
import jax.numpy as jnp
import numpy as np
from jax import lax

D = 768
HEADS = 12
HEAD_DIM = 64
FF = 3072
EXP = 3
CH = 72
PIX = 64
NLEAD = 40
P_SIZE = 1536
FRAMES = 8


def plant(result, rng, least, largest):
    place = [jax.random.randint(jax.random.fold_in(rng, axis), (), 0, length) for axis, length in enumerate(result.shape)]
    widest = result.shape.index(max(result.shape))
    neighbour = place[:widest] + [(place[widest] + 1) % result.shape[widest]] + place[widest + 1:]
    return result.at[tuple(place)].set(least).at[tuple(neighbour)].set(largest)


def level_of(key, dims, pieces, least, largest):
    def one(dim, shards_of):
        steps = jax.random.uniform(jax.random.fold_in(jax.random.fold_in(key, 6), dim), (shards_of,), jnp.float32, least / len(pieces), largest / len(pieces))
        return jnp.repeat(jnp.exp(steps), dims[dim] // shards_of).reshape((-1,) + (1,) * (len(dims) - dim - 1))

    level = one(*pieces[0])
    for cut in pieces[1:]:
        level = level * one(*cut)
    return level


def cumulative_ranks(count, skew):
    loads = [(1 << 20) // math.isqrt(grade ** skew) + 1 for grade in range(1, count + 1)]
    deviation = 1 + sum(loads) // (1 << 30)
    return np.cumsum(np.array([max(1, weight // deviation) for weight in loads]))


def skewed_ids(own_key, dims, count, skew):
    table = cumulative_ranks(count, skew)
    lot = jax.random.randint(jax.random.fold_in(own_key, 1), dims, 0, int(table[count - 1]))
    standing = jnp.searchsorted(jnp.asarray(table, jnp.int32), lot, side="right")
    return jax.random.permutation(jax.random.fold_in(own_key, 2), count)[standing].astype(jnp.int32)


def normal_values(own_key, shape, width, reach, shards=(), kind=jnp.bfloat16):
    level = level_of(own_key, shape, shards, -0.22, 0.18) if shards else 1.0
    values = jax.random.normal(own_key, shape, jnp.float32) * width * level
    return jnp.minimum(jnp.maximum(values, -reach), reach).astype(kind)


def setup_inputs(seed: int = 0) -> dict:
    keys = jax.random.split(jax.random.key(seed), 20)
    fields = normal_values(keys[0], (FRAMES, EXP, CH, PIX, P_SIZE), 1.0, 6.0, ((0, 8), (2, 4)))
    lead_index = plant(skewed_ids(keys[1], (FRAMES,), NLEAD, 2), jax.random.fold_in(keys[1], 3), 0, NLEAD - 1).astype(jnp.int32)
    embed_weight = normal_values(keys[2], (EXP, CH, PIX, D), (EXP * CH * PIX) ** -0.5, 0.0546875, ((1, 4),))
    position_embed = normal_values(keys[3], (P_SIZE, D), 0.5, 3.0, ((0, 4),))
    lead_table = normal_values(keys[4], (NLEAD, D), 0.5, 3.0)
    attend_gain = jnp.clip(1.0 + 0.1 * jax.random.normal(keys[5], (D,), jnp.float32), 0.5, 1.5)
    attend_shift = normal_values(keys[6], (D,), 0.2, 1.2, (), jnp.float32)
    attend_weight = normal_values(keys[7], (D, 3 * D), D ** -0.5, 0.21875)
    out_weight = normal_values(keys[8], (D, D), (D // 16) ** -0.5, 0.875)
    out_bias = normal_values(keys[9], (D,), 0.2, 1.2, (), jnp.float32)
    mixer_gain = jnp.clip(1.0 + 0.1 * jax.random.normal(keys[10], (D,), jnp.float32), 0.5, 1.5)
    mixer_shift = normal_values(keys[11], (D,), 0.2, 1.2, (), jnp.float32)
    up_weight = normal_values(keys[12], (D, FF), D ** -0.5, 0.21875)
    up_bias = normal_values(keys[13], (FF,), 0.2, 1.2, (), jnp.float32)
    down_weight = normal_values(keys[14], (FF, D), FF ** -0.5, 0.109375)
    down_bias = normal_values(keys[15], (D,), 0.2, 1.2, (), jnp.float32)
    head_weight = normal_values(keys[16], (D, EXP * PIX), (4 * D) ** -0.5, 0.109375)
    specialist_cell_offset = normal_values(keys[17], (EXP, CH, PIX), 0.5, 3.0, ((1, 4),), jnp.float32)
    cotangent = normal_values(keys[18], (FRAMES, CH, PIX, P_SIZE), 1.0, 6.0, ((0, 8), (1, 4)))
    return dict(fields=fields, lead_index=lead_index, embed_weight=embed_weight, position_embed=position_embed, lead_table=lead_table, attend_gain=attend_gain, attend_shift=attend_shift, attend_weight=attend_weight, out_weight=out_weight, out_bias=out_bias, mixer_gain=mixer_gain, mixer_shift=mixer_shift, up_weight=up_weight, up_bias=up_bias, down_weight=down_weight, down_bias=down_bias, head_weight=head_weight, specialist_cell_offset=specialist_cell_offset, cotangent=cotangent)


finest_accuracy_mode = lax.Precision.HIGHEST
epsilon = 1e-05

@jax.custom_vjp
def low(v):
    return lax.optimization_barrier(v.astype(jnp.bfloat16)).astype(jnp.float32)

@jax.custom_vjp
def low_back(v):
    return v

def low_keep(v):
    return (low(v), None)

def low_pass(kept, grad):
    return (grad,)

def back_keep(v):
    return (v, None)

def back_low(kept, grad):
    return (low(grad),)
low.defvjp(low_keep, low_pass)
low_back.defvjp(back_keep, back_low)

def layer_norm(v, gain, shift):
    average = lax.optimization_barrier(jnp.mean(v, axis=-1, keepdims=True))
    centred = v - average
    spread = lax.optimization_barrier(jnp.mean(centred * centred, axis=-1, keepdims=True))
    return centred * lax.rsqrt(spread + epsilon) * gain + shift

def frame_forward(params, snapshot_source_variables, lead_onehot):
    embed_weight, position_embed, lead_table, attend_gain, attend_shift, attend_weight, out_weight, out_bias, mixer_gain, mixer_shift, up_weight, up_bias, down_weight, down_bias, head_weight, specialist_cell_offset = params
    embedded = jnp.einsum('ecip,ecid->pd', snapshot_source_variables, embed_weight, precision=finest_accuracy_mode)
    lead_vector = jnp.dot(lead_onehot, lead_table, precision=finest_accuracy_mode)
    stream = low_back(embedded) + position_embed + lead_vector[None, :]
    normed = low(layer_norm(stream, attend_gain, attend_shift))
    packed = low(low_back(jnp.dot(normed, attend_weight, precision=finest_accuracy_mode)))
    queries = packed[:, :D].reshape(P_SIZE, HEADS, HEAD_DIM)
    key_rows = packed[:, D:2 * D].reshape(P_SIZE, HEADS, HEAD_DIM)
    values = packed[:, 2 * D:].reshape(P_SIZE, HEADS, HEAD_DIM)
    scores = low_back(jnp.einsum('qhd,khd->hqk', queries, key_rows, precision=finest_accuracy_mode) * HEAD_DIM ** (-0.5))
    shares = low(jax.nn.softmax(scores, axis=-1))
    attended = low(low_back(jnp.einsum('hqk,khd->qhd', shares, values, precision=finest_accuracy_mode))).reshape(P_SIZE, D)
    stream = stream + low_back(jnp.dot(attended, out_weight, precision=finest_accuracy_mode)) + out_bias
    normed = low(layer_norm(stream, mixer_gain, mixer_shift))
    hidden = low_back(jnp.dot(normed, up_weight, precision=finest_accuracy_mode)) + up_bias
    active = low(jax.nn.gelu(hidden, approximate=True))
    stream = stream + low_back(jnp.dot(active, down_weight, precision=finest_accuracy_mode)) + down_bias
    logits = low_back(jnp.dot(low(stream), head_weight, precision=finest_accuracy_mode))
    specialist_mixing_shares = jax.nn.softmax(logits.reshape(P_SIZE, EXP, PIX), axis=1)
    merged_prediction = snapshot_source_variables + specialist_cell_offset[:, :, :, None]
    return jnp.einsum('msv,sevm->evm', specialist_mixing_shares, merged_prediction, precision=finest_accuracy_mode)

def reference(fields, lead_index, embed_weight, position_embed, lead_table, attend_gain, attend_shift, attend_weight, out_weight, out_bias, mixer_gain, mixer_shift, up_weight, up_bias, down_weight, down_bias, head_weight, specialist_cell_offset, cotangent):
    params = (embed_weight.astype(jnp.float32), position_embed.astype(jnp.float32), lead_table.astype(jnp.float32), attend_gain.astype(jnp.float32), attend_shift.astype(jnp.float32), attend_weight.astype(jnp.float32), out_weight.astype(jnp.float32), out_bias.astype(jnp.float32), mixer_gain.astype(jnp.float32), mixer_shift.astype(jnp.float32), up_weight.astype(jnp.float32), up_bias.astype(jnp.float32), down_weight.astype(jnp.float32), down_bias.astype(jnp.float32), head_weight.astype(jnp.float32), specialist_cell_offset.astype(jnp.float32))
    inputs = fields.astype(jnp.float32)
    onehots = (lead_index[:, None] == jnp.arange(NLEAD, dtype=jnp.int32)[None, :]).astype(jnp.float32)
    frame_step = jax.checkpoint(frame_forward)

    def forward(weights_all, inputs_all):

        def one_frame(frame_items):
            return frame_step(weights_all, frame_items[0], frame_items[1])
        return lax.map(one_frame, (inputs_all, onehots))
    mixed_prediction, pullback = jax.vjp(forward, params, inputs)
    param_grads, source_cotangent = pullback(cotangent.astype(jnp.float32))
    return (mixed_prediction.astype(jnp.bfloat16), source_cotangent.astype(jnp.bfloat16), param_grads[0], param_grads[1], param_grads[2], param_grads[3], param_grads[4], param_grads[5], param_grads[6], param_grads[7], param_grads[8], param_grads[9], param_grads[10], param_grads[11], param_grads[12], param_grads[13], param_grads[14], param_grads[15])
```

```python
from functools import partial

import jax
import jax.numpy as jnp
from jax import lax
from jax.experimental import pallas as pl
from jax.experimental.pallas import tpu as pltpu
from jax.sharding import PartitionSpec as P

HEADS = 12
HEAD_DIM = 64
EXP = 3
PIX = 64
LOG2E = 1.4426950408889634

epsilon = 1e-05
BF = jnp.bfloat16
F32 = jnp.float32


def dot(left, right, left_dim, right_dim):
    return lax.dot_general(
        left, right, (((left_dim,), (right_dim,)), ((), ())), preferred_element_type=F32
    )


class Plan:
    def __init__(self, frames, chan):
        self.frames, self.chan, self.half = frames, chan, chan // 2

    def pairs(self, target):
        return [
            (f * self.chan + z, (lambda t: t[0] * self.chan + t[1])(target(f, z)))
            for f in range(self.frames)
            for z in range(self.chan)
        ]

    def swap_frame(self, x, bit):
        return lax.ppermute(x, ("frames", "chan"), self.pairs(lambda f, z: (f ^ bit, z)))

    def swap_chan(self, x, bit):
        return lax.ppermute(x, ("frames", "chan"), self.pairs(lambda f, z: (f, z ^ bit)))

    def worker(self, f, r):
        return (f & ~1) + r % 2, (f & 1) * self.half + r // 2

    def to_worker(self, x, s):
        return lax.ppermute(
            x, ("frames", "chan"), self.pairs(lambda f, z: self.worker(f, z ^ s))
        )

    def from_worker(self, x, s):
        pairs = self.pairs(lambda f, z: self.worker(f, z ^ s))
        return lax.ppermute(x, ("frames", "chan"), [(d, o) for o, d in pairs])


def bits_of(n):
    return [1 << i for i in range(n.bit_length() - 1)]


def attend_kernel(q_ref, k_ref, v_ref, o_ref, e_ref, rinv_ref):
    scale = HEAD_DIM ** (-0.5) * LOG2E
    for h in range(q_ref.shape[1] // HEAD_DIM):
        cols = slice(h * HEAD_DIM, (h + 1) * HEAD_DIM)
        s = dot(q_ref[:, cols], k_ref[:, cols], 1, 1)
        m = jnp.max(s, axis=1, keepdims=True)
        e = jnp.exp2((s - m) * scale)
        total = jnp.sum(e, axis=1, keepdims=True)
        low = e.astype(BF)
        e_ref[h] = low
        o = dot(low, v_ref[:, cols], 1, 0)
        rinv = jnp.broadcast_to(1.0 / total, o.shape)
        rinv_ref[:, cols] = rinv
        o_ref[:, cols] = (o * rinv).astype(BF)


def attend(q, kv):
    rows, width = q.shape
    keys = kv.shape[0]
    lanes = 2 * HEAD_DIM
    steps = width // lanes
    return pl.pallas_call(
        attend_kernel,
        grid=(steps,),
        in_specs=[
            pl.BlockSpec((rows, lanes), lambda i: (0, i)),
            pl.BlockSpec((keys, lanes), lambda i: (0, i)),
            pl.BlockSpec((keys, lanes), lambda i: (0, i + steps)),
        ],
        out_specs=[
            pl.BlockSpec((rows, lanes), lambda i: (0, i)),
            pl.BlockSpec((2, rows, keys), lambda i: (i, 0, 0)),
            pl.BlockSpec((rows, lanes), lambda i: (0, i)),
        ],
        out_shape=[
            jax.ShapeDtypeStruct((rows, width), BF),
            jax.ShapeDtypeStruct((HEADS, rows, keys), BF),
            jax.ShapeDtypeStruct((rows, width), F32),
        ],
        compiler_params=pltpu.CompilerParams(vmem_limit_bytes=48 << 20),
        cost_estimate=pl.CostEstimate(
            flops=16 * rows * keys * width, bytes_accessed=24 << 20, transcendentals=0
        ),
        name="attend",
    )(q, kv, kv)


def attend_back_kernel(q_ref, k_ref, v_ref, o_ref, do_ref, e_ref, rinv_ref, dq_ref, dk_ref, dv_ref):
    scale = HEAD_DIM ** (-0.5)
    for h in range(q_ref.shape[1] // HEAD_DIM):
        cols = slice(h * HEAD_DIM, (h + 1) * HEAD_DIM)
        do = do_ref[:, cols].astype(F32) * rinv_ref[:, cols]
        inner = jnp.sum(do * o_ref[:, cols].astype(F32), axis=1, keepdims=True)
        do = do.astype(BF)
        e = e_ref[h]
        dp = dot(do, v_ref[:, cols], 1, 1)
        ds = (e.astype(F32) * (dp - inner)).astype(BF)
        dq_ref[:, cols] = (dot(ds, k_ref[:, cols], 1, 0) * scale).astype(BF)
        dk_ref[:, cols] = (dot(ds, q_ref[:, cols], 0, 0) * scale).astype(BF)
        dv_ref[:, cols] = dot(e, do, 0, 0).astype(BF)


def attend_back(q, kv, o, do, e, rinv):
    rows, width = q.shape
    keys = kv.shape[0]
    lanes = 2 * HEAD_DIM
    steps = width // lanes
    row_spec = pl.BlockSpec((rows, lanes), lambda i: (0, i))
    key_spec = pl.BlockSpec((keys, lanes), lambda i: (0, i))
    return pl.pallas_call(
        attend_back_kernel,
        grid=(steps,),
        in_specs=[
            row_spec,
            key_spec,
            pl.BlockSpec((keys, lanes), lambda i: (0, i + steps)),
            row_spec,
            row_spec,
            pl.BlockSpec((2, rows, keys), lambda i: (i, 0, 0)),
            row_spec,
        ],
        out_specs=[row_spec, key_spec, key_spec],
        out_shape=[
            jax.ShapeDtypeStruct((rows, width), BF),
            jax.ShapeDtypeStruct((keys, width), BF),
            jax.ShapeDtypeStruct((keys, width), BF),
        ],
        compiler_params=pltpu.CompilerParams(vmem_limit_bytes=48 << 20),
        cost_estimate=pl.CostEstimate(
            flops=40 * rows * keys * width, bytes_accessed=32 << 20, transcendentals=0
        ),
        name="attend_back",
    )(q, kv, kv, o, do, e, rinv)


def blend_kernel(
    chunk_ref, logit_ref, fields_ref, cot_ref, offset_ref, *rest
):
    mixed_ref, gate_ref, part_ref, bias_ref, total = rest[-5:]
    step = pl.program_id(0)
    channels = cot_ref.shape[0]

    @pl.when(step == 0)
    def _():
        a, b, c = (logit_ref[e * PIX : (e + 1) * PIX, :].astype(F32) for e in range(EXP))
        m = jnp.maximum(jnp.maximum(a, b), c)
        a, b, c = jnp.exp(a - m), jnp.exp(b - m), jnp.exp(c - m)
        scale = 1.0 / (a + b + c)
        for e, x in enumerate((a, b, c)):
            gate_ref[e * PIX : (e + 1) * PIX, :] = x * scale
        total[...] = jnp.zeros_like(total)

    high = 16
    for i in range(0, PIX, high):
        gates = [gate_ref[e * PIX + i : e * PIX + i + high, :] for e in range(EXP)]
        sums = [total[e * PIX + i : e * PIX + i + high, :] for e in range(EXP)]
        for c in range(channels):
            g = cot_ref[c, i : i + high, :].astype(F32)
            mixed = None
            for e in range(EXP):
                x = fields_ref[e, c, i : i + high, :].astype(F32) + offset_ref[e, c, i : i + high, :]
                term = gates[e] * x
                mixed = term if mixed is None else mixed + term
                sums[e] = sums[e] + g * x
                bias_ref[e, c, i : i + high, :] = jnp.sum(gates[e] * g, axis=1, keepdims=True)
            mixed_ref[c, i : i + high, :] = mixed.astype(BF)
        for e in range(EXP):
            total[e * PIX + i : e * PIX + i + high, :] = sums[e]

    @pl.when(step == pl.num_programs(0) - 1)
    def _():
        gates = [gate_ref[e * PIX : (e + 1) * PIX, :] for e in range(EXP)]
        sums = [total[e * PIX : (e + 1) * PIX, :] for e in range(EXP)]
        inner = gates[0] * sums[0] + gates[1] * sums[1] + gates[2] * sums[2]
        for e in range(EXP):
            part_ref[e * PIX : (e + 1) * PIX, :] = (gates[e] * (sums[e] - inner)).astype(BF)


def blend(chunk, logits, fields, cot, offset, mixed):
    channels, pixels, patches = cot.shape
    rows = logits.shape[1]
    block = max(b for b in (6, 3, 2, 1) if channels % b == 0)
    wide = pl.BlockSpec((EXP * PIX, rows), lambda i, r: (0, 0))
    in_specs = [
        wide,
        pl.BlockSpec((EXP, block, PIX, rows), lambda i, r: (0, i, 0, r[0])),
        pl.BlockSpec((block, PIX, rows), lambda i, r: (i, 0, r[0])),
        pl.BlockSpec((EXP, block, PIX, 1), lambda i, r: (0, i, 0, 0)),
    ]
    operands = [chunk, logits, fields, cot, offset]
    aliases = {}
    if mixed is not None:
        in_specs.append(pl.BlockSpec(memory_space=pl.ANY))
        operands.append(mixed)
        aliases = {5: 0}
    return pl.pallas_call(
        blend_kernel,
        grid_spec=pltpu.PrefetchScalarGridSpec(
            num_scalar_prefetch=1,
            grid=(channels // block,),
            in_specs=in_specs,
            out_specs=[
                pl.BlockSpec((block, PIX, rows), lambda i, r: (i, 0, r[0])),
                wide,
                wide,
                pl.BlockSpec((EXP, block, PIX, 1), lambda i, r: (0, i, 0, 0)),
            ],
            scratch_shapes=[pltpu.VMEM((EXP * PIX, rows), F32)],
        ),
        out_shape=[
            jax.ShapeDtypeStruct(cot.shape, BF),
            jax.ShapeDtypeStruct((EXP * PIX, rows), F32),
            jax.ShapeDtypeStruct((EXP * PIX, rows), BF),
            jax.ShapeDtypeStruct((EXP, channels, PIX, 1), F32),
        ],
        input_output_aliases=aliases,
        compiler_params=pltpu.CompilerParams(vmem_limit_bytes=40 << 20),
        cost_estimate=pl.CostEstimate(flops=8 << 20, bytes_accessed=6 << 20, transcendentals=0),
        name="blend",
    )(*operands)


def fields_back_kernel(chunk_ref, weight_ref, start_ref, gate_ref, cot_ref, *rest):
    out_ref = rest[-1]
    grad = dot(weight_ref[0], start_ref[...], 1, 1)
    gate = gate_ref[...]
    for c in range(cot_ref.shape[0]):
        lines = slice(c * PIX, (c + 1) * PIX)
        out_ref[0, lines, :] = (grad[lines, :] + gate * cot_ref[c].astype(F32)).astype(BF)


def fields_back(chunk, weight, start, gates, cot, grad):
    channels, pixels, patches = cot.shape
    rows = gates.shape[1]
    width = weight.shape[2]
    block = max(b for b in (6, 3, 2, 1) if channels % b == 0)
    in_specs = [
        pl.BlockSpec((1, block * PIX, width), lambda e, i, r: (e, i, 0)),
        pl.BlockSpec((rows, width), lambda e, i, r: (0, 0)),
        pl.BlockSpec((PIX, rows), lambda e, i, r: (e, 0)),
        pl.BlockSpec((block, PIX, rows), lambda e, i, r: (i, 0, r[0])),
    ]
    operands = [chunk, weight, start, gates, cot]
    aliases = {}
    if grad is not None:
        in_specs.append(pl.BlockSpec(memory_space=pl.ANY))
        operands.append(grad)
        aliases = {5: 0}
    return pl.pallas_call(
        fields_back_kernel,
        grid_spec=pltpu.PrefetchScalarGridSpec(
            num_scalar_prefetch=1,
            grid=(EXP, channels // block),
            in_specs=in_specs,
            out_specs=pl.BlockSpec((1, block * PIX, rows), lambda e, i, r: (e, i, r[0])),
        ),
        out_shape=jax.ShapeDtypeStruct((EXP, channels * PIX, patches), BF),
        input_output_aliases=aliases,
        compiler_params=pltpu.CompilerParams(vmem_limit_bytes=40 << 20),
        cost_estimate=pl.CostEstimate(
            flops=2 * EXP * channels * PIX * rows * width, bytes_accessed=10 << 20, transcendentals=0
        ),
        name="fields_back",
    )(*operands)


def norm_parts(v):
    centred = v - jnp.mean(v, axis=-1, keepdims=True)
    spread = jnp.mean(centred * centred, axis=-1, keepdims=True)
    r = lax.rsqrt(spread + epsilon)
    return centred * r, r


def norm_back(grad, n, r, gain):
    t = grad * gain
    return r * (
        t - jnp.mean(t, axis=-1, keepdims=True) - n * jnp.mean(t * n, axis=-1, keepdims=True)
    )


def add_low(a, b):
    return (a.astype(F32) + b.astype(F32)).astype(BF)


def halve(x, axis, mine):
    keep = lax.dynamic_index_in_dim(x, mine, axis, keepdims=False)
    send = lax.dynamic_index_in_dim(x, 1 - mine, axis, keepdims=False)
    return keep, send


def frame_levels(plan, x, bits, f):
    left = sorted(bits, reverse=True)
    for bit in bits:
        axis = left.index(bit)
        keep, send = halve(x, axis, (f // bit) % 2)
        x = add_low(keep, plan.swap_frame(send, bit))
        left.remove(bit)
    return x


def chan_levels(plan, x, z):
    bits = bits_of(plan.chan)
    x = x.reshape((2,) * len(bits) + x.shape[1:])
    left = sorted(bits, reverse=True)
    for bit in bits:
        axis = left.index(bit)
        keep, send = halve(x, axis, (z // bit) % 2)
        x = add_low(keep, plan.swap_chan(send, bit))
        left.remove(bit)
    return x


def core_product(plan, left, right, f):
    rows, columns = left.shape
    parts = left.reshape(rows, plan.frames // 2, 2, columns // plan.frames)
    keep, send = halve(parts, 2, f % 2)
    keep, send = (a.reshape(rows, columns // 2) for a in (keep, send))
    far = plan.swap_frame(dot(send, right, 0, 0).astype(BF), 1)
    both = (dot(keep, right, 0, 0) + far.astype(F32)).astype(BF)
    return both.reshape(plan.frames // 2, columns // plan.frames, right.shape[1])


def high_axes(plan, x):
    return x.reshape((2,) * (len(bits_of(plan.frames)) - 1) + x.shape[1:])


def on_device(
    plan,
    fields,
    lead_index,
    embed_weight,
    position_embed,
    lead_table,
    attend_gain,
    attend_shift,
    attend_weight,
    out_weight,
    out_bias,
    mixer_gain,
    mixer_shift,
    up_weight,
    up_bias,
    down_weight,
    down_bias,
    head_weight,
    specialist_cell_offset,
    cotangent,
):
    f, z = lax.axis_index("frames"), lax.axis_index("chan")
    chan, frames = plan.chan, plan.frames
    width = attend_gain.shape[0]
    channels, pixels, patches = cotangent.shape[1:]
    rows = position_embed.shape[0]
    lines = EXP * channels * PIX
    own_fields, cot = fields[0], cotangent[0]
    flat_fields = own_fields.reshape(lines, patches)
    flat_weight = embed_weight.reshape(lines, width)

    onehot = (
        lead_index[:, None] == jnp.arange(lead_table.shape[0], dtype=jnp.int32)[None, :]
    ).astype(BF)
    lead_vector = dot(onehot, lead_table, 1, 0)
    got = []
    for s in range(chan):
        block = lax.dynamic_slice(flat_fields, (0, (z ^ s) * rows), (lines, rows))
        part = dot(block, flat_weight, 0, 0)
        if s == 0:
            part = part + position_embed.astype(F32) + lead_vector
        got.append(plan.to_worker(part.astype(BF), s))
    stream_start = sum(a.astype(F32) for a in got)

    first_n, first_r = norm_parts(stream_start)
    normed_first = (first_n * attend_gain + attend_shift).astype(BF)
    chunks = [normed_first]
    for bit in bits_of(plan.half):
        chunks += [plan.swap_chan(a, bit) for a in chunks]
    every = []
    for a in chunks:
        every += [a, plan.swap_frame(a, 1)]
    normed_every = jnp.concatenate(every, axis=0)
    queries = dot(normed_first, attend_weight[:, :width], 1, 0).astype(BF)
    keys_values = dot(normed_every, attend_weight[:, width:], 1, 0).astype(BF)
    attended, shares, rinv = attend(queries, keys_values)

    stream_mid = stream_start + dot(attended, out_weight, 1, 0) + out_bias
    second_n, second_r = norm_parts(stream_mid)
    normed_second = (second_n * mixer_gain + mixer_shift).astype(BF)
    hidden = dot(normed_second, up_weight, 1, 0) + up_bias
    active = jax.nn.gelu(hidden, approximate=True).astype(BF)
    end_low = (stream_mid + dot(active, down_weight, 1, 0) + down_bias).astype(BF)
    logits = dot(head_weight, end_low, 0, 1).astype(BF)

    offset = specialist_cell_offset[..., None]
    numbers = [(z ^ s).astype(jnp.int32)[None] for s in range(chan)]
    near = [plan.from_worker(logits, s) for s in range(chan)]
    mixed, gates, bias_parts, back = None, [], [], []
    for s in range(chan):
        mixed, gate, part, bias = blend(numbers[s], near[s], own_fields, cot, offset, mixed)
        gates.append(gate)
        bias_parts.append(bias)
        back.append(plan.to_worker(part, s))
    expert_bias = sum(bias_parts)[..., 0]
    logit_low = sum(a.astype(F32) for a in back).astype(BF)

    end_grad = dot(logit_low, head_weight, 0, 1)
    down_bias_grad = jnp.sum(end_grad, axis=0)
    down_low = end_grad.astype(BF)
    active_grad = dot(down_low, down_weight, 1, 1)
    gelu_pull = jax.vjp(partial(jax.nn.gelu, approximate=True), hidden)[1]
    hidden_grad = gelu_pull(active_grad)[0]
    up_bias_grad = jnp.sum(hidden_grad, axis=0)
    hidden_low = hidden_grad.astype(BF)
    second_grad = dot(hidden_low, up_weight, 1, 1)
    mixer_gain_grad = jnp.sum(second_grad * second_n, axis=0)
    mixer_shift_grad = jnp.sum(second_grad, axis=0)
    mid_grad = end_grad + norm_back(second_grad, second_n, second_r, mixer_gain)
    out_bias_grad = jnp.sum(mid_grad, axis=0)
    branch_low = mid_grad.astype(BF)
    attended_low = dot(branch_low, out_weight, 1, 1).astype(BF)

    query_low, key_low, value_low = attend_back(
        queries, keys_values, attended, attended_low, shares, rinv
    )
    key_value_low = jnp.concatenate([key_low, value_low], axis=1)
    far_grad = dot(key_value_low, attend_weight[:, width:], 1, 1)
    parts = [far_grad[i * rows : (i + 1) * rows] for i in range(chan)]
    parts[0] = parts[0] + dot(query_low, attend_weight[:, :width], 1, 1)
    parts = [
        parts[2 * i] + plan.swap_frame(parts[2 * i + 1].astype(BF), 1).astype(F32)
        for i in range(plan.half)
    ]
    for bit in reversed(bits_of(plan.half)):
        parts = [
            parts[i] + plan.swap_chan(parts[i + bit].astype(BF), bit).astype(F32)
            for i in range(bit)
        ]
    first_grad = parts[0]
    attend_gain_grad = jnp.sum(first_grad * first_n, axis=0)
    attend_shift_grad = jnp.sum(first_grad, axis=0)
    start_grad = mid_grad + norm_back(first_grad, first_n, first_r, attend_gain)

    vectors = jnp.stack(
        [
            attend_gain_grad,
            attend_shift_grad,
            mixer_gain_grad,
            mixer_shift_grad,
            out_bias_grad,
            down_bias_grad,
        ]
    )
    n_up = up_bias.shape[0] // width
    vectors = jnp.concatenate([vectors, up_bias_grad.reshape(width, n_up).T], axis=0)
    n_vectors = vectors.shape[0]
    vectors = jnp.pad(vectors, ((0, 16 - n_vectors), (0, 0)))
    sent = jnp.concatenate([start_grad, vectors], axis=0).astype(BF)
    got = [plan.from_worker(sent, s) for s in range(chan)]
    fields_grad = None
    for s in range(chan):
        fields_grad = fields_back(
            numbers[s], embed_weight.reshape(EXP, channels * PIX, width), got[s], gates[s], cot, fields_grad
        )
    ordered = []
    for r in range(chan):
        choice = got[0]
        for s in range(1, chan):
            choice = jnp.where(z == r ^ s, got[s], choice)
        ordered.append(choice[:rows])
    start_every = jnp.concatenate(ordered, axis=0)
    vector_sum = sum(a[rows:].astype(F32) for a in got)
    lead_sum = jnp.sum(start_every.astype(F32), axis=0)

    per = width // frames
    small = jnp.concatenate(
        [vector_sum, onehot[0].astype(F32)[:, None] * lead_sum[None, :]], axis=0
    )
    n_small = small.shape[0]
    n_bias = EXP * channels
    bias_here = expert_bias.reshape(n_bias, frames, PIX // frames)
    bias_here = jnp.pad(
        jnp.transpose(bias_here, (1, 2, 0)), ((0, 0), (0, per - PIX // frames), (0, 0))
    )
    extra = jnp.concatenate(
        [got[0][:rows].T, small.T.astype(BF), bias_here.reshape(width, n_bias).astype(BF)], axis=1
    )
    extra = jnp.pad(extra, ((0, 0), (0, -extra.shape[1] % 128)))
    n_extra = extra.shape[1]
    embed_sum = core_product(plan, start_every, flat_fields.T, f)
    keep, send = halve(extra.reshape(frames // 2, 2, per, n_extra), 1, f % 2)
    extra = add_low(keep, plan.swap_frame(send, 1))
    high = bits_of(frames)[1:]
    cut = (lines + n_extra) // 256 * 128
    parts = [embed_sum[:, :, :cut], jnp.concatenate([embed_sum[:, :, cut:], extra], axis=2)]
    parts = [
        frame_levels(plan, high_axes(plan, a), order, f)
        for a, order in zip(parts, (high, high[::-1]))
    ]
    tail = jnp.concatenate(parts, axis=1).astype(F32)
    embed_out = tail[:, :lines].T.reshape(EXP, channels, PIX, per)
    position_out = tail[:, lines : lines + rows].T
    small_out = lax.dynamic_slice_in_dim(
        tail[:, lines + rows : lines + rows + n_small], z * (per // chan), per // chan, 0
    )
    vectors_out = [small_out[:, i] for i in range(6)]
    up_bias_out = small_out[:, 6 : 6 + n_up].reshape(-1)
    table_out = small_out[:, 16:].T
    bias_out = tail[: PIX // frames, lines + rows + n_small : lines + rows + n_small + n_bias]
    bias_out = bias_out.T.reshape(EXP, channels, PIX // frames)

    down_sum = core_product(plan, active, down_low, f)
    wide_sum = [
        core_product(plan, normed_second, hidden_low, f),
        core_product(plan, attended, branch_low, f),
        core_product(plan, end_low, logit_low.T, f),
    ]
    wide_sum = jnp.concatenate(wide_sum, axis=2)
    attend_sum = jnp.concatenate(
        [
            core_product(plan, normed_first, query_low, f),
            core_product(plan, normed_every, key_value_low, f),
        ],
        axis=2,
    )
    down_sum = frame_levels(plan, high_axes(plan, down_sum), high, f)
    wide_sum = frame_levels(plan, high_axes(plan, wide_sum), high[::-1], f)
    cut = attend_sum.shape[2] // 2
    attend_sum = jnp.concatenate(
        [
            frame_levels(plan, high_axes(plan, attend_sum[:, :, :cut]), high, f),
            frame_levels(plan, high_axes(plan, attend_sum[:, :, cut:]), high[::-1], f),
        ],
        axis=1,
    )
    down_sum = chan_levels(plan, down_sum.reshape(chan, -1, width), z).astype(F32)
    wide_sum = chan_levels(plan, wide_sum.reshape(chan, -1, wide_sum.shape[1]), z).astype(F32)
    attend_sum = chan_levels(plan, attend_sum.reshape(chan, -1, 3 * width), z).astype(F32)
    n_ff = up_bias.shape[0]

    return (
        mixed[None],
        fields_grad.reshape(fields.shape),
        embed_out,
        position_out,
        table_out,
        vectors_out[0],
        vectors_out[1],
        attend_sum,
        wide_sum[:, n_ff : n_ff + width],
        vectors_out[4],
        vectors_out[2],
        vectors_out[3],
        wide_sum[:, :n_ff],
        up_bias_out,
        down_sum,
        vectors_out[5],
        wide_sum[:, n_ff + width :],
        bias_out,
    )


def solution(mesh):
    plan = Plan(mesh.shape["frames"], mesh.shape["chan"])
    both = ("frames", "chan")
    in_specs = (
        P("frames", None, "chan", None, None),
        P("frames"),
        P(None, "chan", None, None),
        P("chan", None),
        *[P()] * 13,
        P(None, "chan", None),
        P("frames", "chan", None, None),
    )
    out_specs = (
        P("frames", "chan", None, None),
        P("frames", None, "chan", None, None),
        P(None, "chan", None, "frames"),
        P("chan", "frames"),
        P(None, both),
        P(both),
        P(both),
        P(both, None),
        P(both, None),
        P(both),
        P(both),
        P(both),
        P(both, None),
        P(both),
        P(both, None),
        P(both),
        P(both, None),
        P(None, "chan", "frames"),
    )
    return jax.shard_map(
        partial(on_device, plan), mesh=mesh, in_specs=in_specs, out_specs=out_specs, check_vma=False
    )
```

```python
from functools import partial

import jax
import jax.numpy as jnp
from jax import lax
from jax.experimental import pallas as pl
from jax.experimental.pallas import tpu as pltpu
from jax.sharding import PartitionSpec as P

HEADS = 12
HEAD_DIM = 64
EXP = 3
PIX = 64
LOG2E = 1.4426950408889634

epsilon = 1e-05
BF = jnp.bfloat16
F32 = jnp.float32


def dot(left, right, left_dim, right_dim):
    return lax.dot_general(
        left, right, (((left_dim,), (right_dim,)), ((), ())), preferred_element_type=F32
    )


class Plan:
    def __init__(self, frames, chan):
        self.frames, self.chan, self.half = frames, chan, chan // 2

    def pairs(self, target):
        return [
            (f * self.chan + z, (lambda t: t[0] * self.chan + t[1])(target(f, z)))
            for f in range(self.frames)
            for z in range(self.chan)
        ]

    def swap_frame(self, x, bit):
        return lax.ppermute(x, ("frames", "chan"), self.pairs(lambda f, z: (f ^ bit, z)))

    def swap_chan(self, x, bit):
        return lax.ppermute(x, ("frames", "chan"), self.pairs(lambda f, z: (f, z ^ bit)))

    def worker(self, f, r):
        return (f & ~1) + r % 2, (f & 1) * self.half + r // 2

    def to_worker(self, x, s):
        return lax.ppermute(
            x, ("frames", "chan"), self.pairs(lambda f, z: self.worker(f, z ^ s))
        )

    def from_workers(self, pair):
        return [
            lax.ppermute(x, ("frames", "chan"), self.sources(lambda f, z: self.holder(f, z, i)))
            for i, x in enumerate((pair, pair))
        ]

    def holder(self, f, z, i):
        return (f & ~1) + z // self.half, (f & 1) * self.half + (z + i) % self.half

    def sources(self, source):
        return [(a, b) for b, a in self.pairs(source)]


def bits_of(n):
    return [1 << i for i in range(n.bit_length() - 1)]


VMEM = 56 << 20


def call(kernel, name, out_shape, in_specs, out_specs, grid=(), scratch=(), scalars=0, cost=0, after=(), **more):
    n_in = scalars + len(in_specs)

    def body(*refs):
        kernel(*refs[:n_in], *refs[n_in + len(after) :])

    run = pl.pallas_call(
        body,
        grid_spec=pltpu.PrefetchScalarGridSpec(
            num_scalar_prefetch=scalars,
            grid=grid,
            in_specs=[*in_specs, *[pl.BlockSpec(memory_space=pl.ANY) for _ in after]],
            out_specs=out_specs,
            scratch_shapes=scratch,
        ),
        out_shape=out_shape,
        compiler_params=pltpu.CompilerParams(vmem_limit_bytes=VMEM),
        cost_estimate=pl.CostEstimate(flops=1 + cost * 10**9, bytes_accessed=1, transcendentals=0),
        name=name,
        **more,
    )
    return lambda *operands: run(*operands, *after)


def shape(*dims, kind=BF):
    return jax.ShapeDtypeStruct(dims, kind)


def whole(x):
    return pl.BlockSpec(x.shape, lambda *_: (0,) * len(x.shape))


def first_norm_kernel(a_ref, b_ref, c_ref, d_ref, gain_ref, shift_ref, start_ref, normed_ref):
    start = sum(x[...].astype(F32) for x in (a_ref, b_ref, c_ref, d_ref))
    start_ref[...] = start
    n, _ = norm_parts(start)
    normed_ref[...] = (n * gain_ref[...] + shift_ref[...]).astype(BF)


def first_norm(parts, gain, shift, after):
    rows, width = parts[0].shape
    operands = [*parts, gain[None], shift[None]]
    out_shape = [shape(rows, width, kind=F32), shape(rows, width)]
    return call(
        first_norm_kernel,
        "first_norm",
        out_shape,
        [whole(a) for a in operands],
        [whole(a) for a in out_shape],
        after=after,
    )(*operands)


def project_kernel(first, near_ref, far_ref, weight_ref, kv_ref, turned_ref, *rest):
    rows = near_ref.shape[0]
    pairs, _, lanes = kv_ref.shape
    step = pl.program_id(0)

    def put():
        for i, x_ref in enumerate((near_ref, far_ref)):
            x = dot(x_ref[...], weight_ref[...], 1, 0).astype(BF)
            for p in range(pairs):
                kv_ref[p, i * rows : (i + 1) * rows, :] = x[:, p * lanes : (p + 1) * lanes]

    @pl.when(step == 0)
    def _():
        for i, x_ref in enumerate((near_ref, far_ref)):
            turned_ref[:, i * rows : (i + 1) * rows] = x_ref[...].T

    if first:

        @pl.when(step == 0)
        def _():
            rest[0][...] = dot(near_ref[...], weight_ref[...], 1, 0).astype(BF)

        pl.when(step > 0)(put)
    else:
        put()


def project(near, far, weight, first, after):
    rows, width = near.shape
    pair = 2 * HEAD_DIM
    pairs = width // pair
    skip = 0 if first else 1
    out_shape = [shape(2 * pairs, 2 * rows, pair), shape(width, 2 * rows)]
    out_specs = [
        pl.BlockSpec((pairs, 2 * rows, pair), lambda i: (jnp.maximum(i + skip - 1, 0), 0, 0)),
        whole(out_shape[1]),
    ]
    if first:
        out_shape.append(shape(rows, width))
        out_specs.append(whole(out_shape[2]))
    return call(
        partial(project_kernel, first),
        "project",
        out_shape,
        [whole(near), whole(far), pl.BlockSpec((width, width), lambda i: (0, i + skip))],
        out_specs,
        grid=(3 - skip,),
        after=after,
    )(near, far, weight)


def attend_kernel(
    q_ref, near_ref, far_ref, near_value_ref, far_value_ref, o_ref, turned_ref, e_ref, rinv_ref
):
    scale = HEAD_DIM ** (-0.5) * LOG2E
    lanes = q_ref.shape[1]
    for h in range(lanes // HEAD_DIM):
        cols = slice(h * HEAD_DIM, (h + 1) * HEAD_DIM)
        q = q_ref[:, cols]
        s_near = dot(q, near_ref[0, :, cols], 1, 1)
        s_far = dot(q, far_ref[0, :, cols], 1, 1)
        m = jnp.maximum(
            jnp.max(s_near, axis=1, keepdims=True), jnp.max(s_far, axis=1, keepdims=True)
        )
        e_near = jnp.exp2((s_near - m) * scale)
        e_far = jnp.exp2((s_far - m) * scale)
        total = jnp.sum(e_near, axis=1, keepdims=True) + jnp.sum(e_far, axis=1, keepdims=True)
        e_near, e_far = e_near.astype(BF), e_far.astype(BF)
        keys = e_near.shape[1]
        e_ref[h, :, :keys] = e_near
        e_ref[h, :, keys:] = e_far
        o = dot(e_near, near_value_ref[0, :, cols], 1, 0) + dot(e_far, far_value_ref[0, :, cols], 1, 0)
        rinv = jnp.broadcast_to(1.0 / total, o.shape)
        rinv_ref[:, cols] = rinv
        o_ref[:, cols] = (o * rinv).astype(BF)
    turned_ref[...] = o_ref[...].T


def attend(q, near, far):
    rows, width = q.shape
    keys = near.shape[1]
    lanes = 2 * HEAD_DIM
    steps = width // lanes
    row_spec = pl.BlockSpec((rows, lanes), lambda i: (0, i))
    key_spec = pl.BlockSpec((1, keys, lanes), lambda i: (i, 0, 0))
    value_spec = pl.BlockSpec((1, keys, lanes), lambda i: (i + steps, 0, 0))
    e_spec = pl.BlockSpec((2, rows, 2 * keys), lambda i: (i, 0, 0))
    return call(
        attend_kernel,
        "attend",
        [
            shape(rows, width),
            shape(width, rows),
            shape(HEADS, rows, 2 * keys),
            shape(rows, width, kind=F32),
        ],
        [row_spec, key_spec, key_spec, value_spec, value_spec],
        [row_spec, pl.BlockSpec((lanes, rows), lambda i: (i, 0)), e_spec, row_spec],
        grid=(steps,),
    )(q, near, far, near, far)


def attend_back_kernel(
    q_ref, near_ref, far_ref, near_value_ref, far_value_ref, o_ref, do_ref, e_ref, rinv_ref,
    dq_ref, keep_ref, send_ref,
):
    scale = HEAD_DIM ** (-0.5)
    rows, lanes = q_ref.shape
    for h in range(lanes // HEAD_DIM):
        cols = slice(h * HEAD_DIM, (h + 1) * HEAD_DIM)
        q = q_ref[:, cols]
        do = do_ref[:, cols].astype(F32) * rinv_ref[:, cols]
        inner = jnp.sum(do * o_ref[:, cols].astype(F32), axis=1, keepdims=True)
        do = do.astype(BF)
        dq = None
        for i, (k_ref, v_ref) in enumerate(((near_ref, near_value_ref), (far_ref, far_value_ref))):
            keys = k_ref.shape[1]
            e = e_ref[h, :, i * keys : (i + 1) * keys]
            dp = dot(do, v_ref[0, :, cols], 1, 1)
            ds = (e.astype(F32) * (dp - inner)).astype(BF)
            part = dot(ds, k_ref[0, :, cols], 1, 0)
            dq = part if dq is None else dq + part
            dk = (dot(ds, q, 0, 0) * scale).astype(BF)
            dv = dot(e, do, 0, 0).astype(BF)
            lines = slice(i * rows, (i + 1) * rows)
            for k, x in enumerate((dk, dv)):
                keep_ref[k, 0, lines, cols] = x[:rows]
                send_ref[k, 0, lines, cols] = x[rows:]
        dq_ref[:, cols] = (dq * scale).astype(BF)


def attend_back(q, near, far, o, do, e, rinv, after):
    rows, width = q.shape
    keys = near.shape[1]
    lanes = 2 * HEAD_DIM
    steps = width // lanes
    row_spec = pl.BlockSpec((rows, lanes), lambda i: (0, i))
    key_spec = pl.BlockSpec((1, keys, lanes), lambda i: (i, 0, 0))
    value_spec = pl.BlockSpec((1, keys, lanes), lambda i: (i + steps, 0, 0))
    e_spec = pl.BlockSpec((2, rows, 2 * keys), lambda i: (i, 0, 0))
    return call(
        attend_back_kernel,
        "attend_back",
        [shape(rows, width), *[shape(2, steps, keys, lanes)] * 2],
        [row_spec, key_spec, key_spec, value_spec, value_spec, row_spec, row_spec, e_spec, row_spec],
        [row_spec, *[pl.BlockSpec((2, 1, keys, lanes), lambda i: (0, i, 0, 0))] * 2],
        grid=(steps,),
        after=after,
    )(q, near, far, near, far, o, do, e, rinv)


def all_pairs(ref, k):
    return jnp.concatenate([ref[k, p] for p in range(ref.shape[1])], axis=1)


def project_back_kernel(grad_ref, weight_ref, *rest):
    step, out_ref = pl.program_id(0), rest[-1]

    @pl.when(step < 2)
    def _():
        x = dot(all_pairs(grad_ref, 0), weight_ref[...], 1, 1)

        @pl.when(step == 0)
        def _():
            rest[-2][...] = x

        @pl.when(step == 1)
        def _():
            out_ref[...] = (rest[-2][...] + x).astype(out_ref.dtype)

    if len(rest) > 2:

        @pl.when(step == 2)
        def _():
            rows = rest[0].shape[0]
            out_ref[:rows, :] += dot(rest[0][...], weight_ref[...], 1, 1)


def project_back(grads, weight, after, *queries):
    _, pairs, rows, lanes = grads.shape
    width = weight.shape[0]
    out_shape = shape(rows, width, kind=F32 if queries else BF)

    def kernel(*refs):
        *ins, out_ref, total = refs
        project_back_kernel(*ins, total, out_ref)

    return call(
        kernel,
        "project_back",
        out_shape,
        [
            pl.BlockSpec((1, pairs, rows, lanes), lambda i: (jnp.minimum(i, 1), 0, 0, 0)),
            pl.BlockSpec((width, width), lambda i: (0, (i + 1) % 3)),
            *[whole(a) for a in queries],
        ],
        whole(out_shape),
        grid=(3 if queries else 2,),
        scratch=[pltpu.VMEM((rows, width), F32)],
        after=after,
    )(grads, weight, *queries)


def relay_kernel(*refs):
    n = len(refs) // 2
    for a, b in zip(refs[:n], refs[n:]):
        b[...] = a[...]


def relay(arrays, after):
    specs = [whole(x) for x in arrays]
    return call(relay_kernel, "relay", [shape(*x.shape) for x in arrays], specs, specs, after=after)(*arrays)


def beside_kernel(core_ref, x_ref, other_ref, out_ref):
    n = x_ref.shape[1]
    for core, (a_ref, b_ref) in enumerate(((x_ref, other_ref), (other_ref, x_ref))):

        @pl.when(core_ref[0] == core)
        def _():
            out_ref[:, :n] = a_ref[...]
            out_ref[:, n:] = b_ref[...]


def beside(core, x, other, after):
    out_shape = shape(x.shape[0], 2 * x.shape[1])
    return call(
        beside_kernel, "beside", out_shape, [whole(x), whole(other)], whole(out_shape), scalars=1, after=after
    )(core, x, other)


def plus_kernel(a_ref, b_ref, out_ref):
    out_ref[...] = (a_ref[...].astype(F32) + b_ref[...].astype(F32)).astype(BF)


def plus(a, b, after):
    return call(plus_kernel, "plus", shape(*a.shape), [whole(a), whole(b)], whole(a), after=after)(a, b)


def middle_kernel(
    start_ref, attended_ref, out_ref, vector_ref, head_ref, pull0_ref, pull1_ref, pull2_ref, pull3_ref, up_any, down_any,
    gate_ref, sum_ref, mid_grad_ref, attended_low_ref, normed_turned_ref, end_turned_ref,
    down_low_ref, logit_low_ref, branch_low_ref, active_any, hidden_any,
    up, down, slope, active_turned, hidden_low, in_sem, out_sem,
):
    rows, width = start_ref.shape
    hidden_width = up.shape[1]
    steps = in_sem.shape[1]
    tile = hidden_width // steps
    tiles = [slice(i * tile, (i + 1) * tile) for i in range(steps)]
    ups = [pltpu.make_async_copy(up_any.at[:, t], up.at[:, t], in_sem.at[0, i]) for i, t in enumerate(tiles)]
    downs = [pltpu.make_async_copy(down_any.at[t], down.at[t], in_sem.at[1, i]) for i, t in enumerate(tiles)]
    outs = [
        pltpu.make_async_copy(active_turned.at[t], active_any.at[t], out_sem.at[0, i])
        for i, t in enumerate(tiles)
    ] + [
        pltpu.make_async_copy(hidden_low.at[:, t], hidden_any.at[:, t], out_sem.at[1, i])
        for i, t in enumerate(tiles)
    ]
    for a, b in zip(ups, downs):
        a.start()
        b.start()
    out_bias, gain, shift, down_bias, up_bias = (
        vector_ref[:, width * i : width * (i + 1) if i < 4 else width * 4 + hidden_width] for i in range(5)
    )
    mid = start_ref[...] + dot(attended_ref[...], out_ref[...], 1, 0) + out_bias
    n, r = norm_parts(mid)
    normed = (n * gain + shift).astype(BF)
    normed_turned_ref[...] = normed.T
    end = mid + down_bias
    k, cube = 0.7978845608028654, 0.044715
    for i, t in enumerate(tiles):
        ups[i].wait()
        h = dot(normed, up[:, t], 1, 0) + up_bias[:, t]
        square = h * h
        th = jnp.tanh(h * (k + (k * cube) * square))
        half = 0.5 + 0.5 * th
        active = (h * half).astype(BF)
        slope[:, t] = half + h * (half * (1.0 - th)) * (k + (3 * k * cube) * square)
        active_turned[t, :] = active.T
        outs[i].start()
        downs[i].wait()
        end = end + dot(active, down[t, :], 1, 0)
    end_low = end.astype(BF)
    end_turned_ref[...] = end_low.T

    logits = dot(end_low, head_ref[...], 1, 0).T
    a, b, c = (logits[e * PIX : (e + 1) * PIX] for e in range(EXP))
    m = jnp.maximum(jnp.maximum(a, b), c)
    a, b, c = jnp.exp(a - m), jnp.exp(b - m), jnp.exp(c - m)
    share = 1.0 / (a + b + c)
    a, b, c = a * share, b * share, c * share
    pull = sum(x[...].astype(F32) for x in (pull0_ref, pull1_ref, pull2_ref, pull3_ref))
    second, third = pull[:PIX], pull[PIX:]
    inner = b * second + c * third
    logit_grad = jnp.concatenate([-a * inner, b * (second - inner), c * (third - inner)], axis=0)
    gate_ref[: EXP * PIX, :] = jnp.concatenate([a, b, c], axis=0).astype(BF)
    logit_low_ref[...] = logit_grad.astype(BF)

    end_grad = dot(logit_grad.T.astype(BF), head_ref[...], 1, 1)
    down_low = end_grad.astype(BF)
    down_low_ref[...] = down_low
    second_grad = jnp.zeros((rows, width), F32)
    per = width // rows
    for i, t in enumerate(tiles):
        grad = dot(down_low, down[t, :], 1, 1) * slope[:, t]
        total = jnp.sum(grad, axis=0, keepdims=True)
        for j in range(tile // rows):
            line = 4 * per + (t.start // rows) + j
            sum_ref[line : line + 1, :] = total[:, j * rows : (j + 1) * rows]
        low = grad.astype(BF)
        hidden_low[:, t] = low
        outs[steps + i].start()
        second_grad = second_grad + dot(low, up[:, t], 1, 1)
    mid_grad = end_grad + norm_back(second_grad, n, r, gain)
    mid_grad_ref[...] = mid_grad
    branch = mid_grad.astype(BF)
    branch_low_ref[...] = branch
    attended_low_ref[...] = dot(branch, out_ref[...], 1, 1).astype(BF)
    for i, x in enumerate((second_grad * n, second_grad, mid_grad, end_grad)):
        x = jnp.sum(x, axis=0, keepdims=True)
        for j in range(per):
            sum_ref[i * per + j : i * per + j + 1, :] = x[:, j * rows : (j + 1) * rows]
    gate_ref[EXP * PIX :, :] = sum_ref[...].astype(BF)
    for a in outs:
        a.wait()


def middle(start, attended, out_w, vectors, head_w, pulls, up_w, down_w):
    rows, width = start.shape
    hidden_width = up_w.shape[1]
    steps = 4
    lines = (4 * width + hidden_width) // rows
    operands = [start, attended, out_w, vectors, head_w, *pulls]
    out_shape = [
        shape(EXP * PIX + lines, rows),
        shape(lines, rows, kind=F32),
        shape(rows, width, kind=F32),
        shape(rows, width),
        shape(width, rows),
        shape(width, rows),
        shape(rows, width),
        shape(EXP * PIX, rows),
        shape(rows, width),
        shape(hidden_width, rows),
        shape(rows, hidden_width),
    ]
    any_spec = pl.BlockSpec(memory_space=pl.ANY)
    return call(
        middle_kernel,
        "middle",
        out_shape,
        [*[whole(a) for a in operands], any_spec, any_spec],
        [*[whole(a) for a in out_shape[:-2]], any_spec, any_spec],
        scratch=[
            pltpu.VMEM((width, hidden_width), BF),
            pltpu.VMEM((hidden_width, width), BF),
            pltpu.VMEM((rows, hidden_width), F32),
            pltpu.VMEM((hidden_width, rows), BF),
            pltpu.VMEM((rows, hidden_width), BF),
            pltpu.SemaphoreType.DMA((2, steps)),
            pltpu.SemaphoreType.DMA((2, steps)),
        ],
    )(*operands, up_w, down_w)


def half_rows(x, blocks, mine, flip):
    per = x.shape[0] // blocks
    x = x.reshape(blocks // 2, 2, per, x.shape[1])
    block = (blocks // 2, 1, per, x.shape[3])
    if per % 16 == 0:
        return x, pl.BlockSpec(block, lambda *a: (0, a[-1][0] ^ flip, 0, 0))
    x = lax.dynamic_index_in_dim(x, mine[0] ^ flip, 1, keepdims=False).reshape(1, 1, -1, x.shape[3])
    return x, whole(x)


def rows_of(ref):
    return ref[...].reshape(-1, ref.shape[3])


def both_halves(send_ref, keep_ref):
    return jnp.concatenate([rows_of(send_ref), rows_of(keep_ref)], axis=0)


def tall_grads_kernel(frames, chan, active_ref, down_ref, out_ref):
    lines, width = active_ref.shape[0], down_ref.shape[1]
    x = dot(active_ref[...], down_ref[...], 1, 0)
    across = out_ref.shape[1] // width
    per = lines // (chan * across * frames)
    parts = [
        jnp.concatenate([x[i + k * per : i + (k + 1) * per] for k in range(across)], axis=1)
        for i in range(0, lines, per * across)
    ]
    out_ref[...] = jnp.concatenate(parts, axis=0).astype(BF)


def tall_grads(frames, chan, active, down, wide, after):
    hidden_width, rows = active.shape
    width = down.shape[1]
    at_once = max(1, frames // 4)
    across = hidden_width // width
    return call(
        partial(tall_grads_kernel, at_once, chan),
        "tall_grads",
        shape(width, hidden_width + wide),
        [pl.BlockSpec((at_once * hidden_width // frames, rows), lambda i: (i, 0)), whole(down)],
        pl.BlockSpec((at_once * width // frames, across * width), lambda i: (i, 0)),
        grid=(frames // at_once,),
        after=after,
    )(active, down)


def wide_grads_kernel(normed_ref, hidden_ref, attended_ref, branch_ref, end_ref, logit_ref, tall_ref, out_ref):
    step, last = pl.program_id(0), pl.num_programs(0) - 1

    @pl.when(step < last)
    def _():
        out_ref[...] = dot(normed_ref[...], hidden_ref[...], 1, 0).astype(BF)

    @pl.when(step == last)
    def _():
        x = dot(attended_ref[...], branch_ref[...], 1, 0)
        y = dot(end_ref[...], logit_ref[...], 1, 1)
        spare = out_ref.shape[1] - x.shape[1] - y.shape[1]
        out_ref[...] = jnp.concatenate([x, y, jnp.zeros((x.shape[0], spare), F32)], axis=1).astype(BF)


WIDE = 1024


def wide_grads(normed, hidden, attended, branch, end, logit, tall):
    width, rows = normed.shape
    hidden_width = hidden.shape[1]
    steps = hidden_width // WIDE + 1
    operands = [normed, hidden, attended, branch, end, logit, tall]
    specs = [whole(x) for x in operands]
    specs[1] = pl.BlockSpec((rows, WIDE), lambda i: (0, jnp.minimum(i, steps - 2)))
    specs[6] = pl.BlockSpec(memory_space=pl.ANY)
    return call(
        wide_grads_kernel,
        "wide_grads",
        shape(*tall.shape),
        specs,
        pl.BlockSpec((width, WIDE), lambda i: (0, i + hidden_width // WIDE)),
        grid=(steps,),
        input_output_aliases={6: 0},
    )(*operands)


def attend_grads_kernel(
    side_ref, near_ref, near2_ref, far_ref, far2_ref, query_ref, keep_grad_ref, send_grad_ref, *rest
):
    sends, keep_ref = rest[:-1], rest[-1]
    rows, width = query_ref.shape
    half = keep_ref.shape[0]
    step = pl.program_id(0)
    near, far = both_halves(near_ref, near2_ref), both_halves(far_ref, far2_ref)

    def put(i, x):
        @pl.when(step == i)
        def _():
            sends[i][...] = x[:half].astype(BF)

        keep_ref[...] = x[half:].astype(BF)

    @pl.when(step == 0)
    def _():
        put(0, dot(near[:, :rows], query_ref[...], 1, 0))

    @pl.when(step > 0)
    def _():
        a, b = all_pairs(keep_grad_ref, 0), all_pairs(send_grad_ref, 0)
        x = dot(near[:, :rows], a[:rows], 1, 0) + dot(near[:, rows:], b[:rows], 1, 0)
        x = x + dot(far[:, :rows], a[rows:], 1, 0) + dot(far[:, rows:], b[rows:], 1, 0)
        put(1, x)
        put(2, x)


def attend_grads(frames, mine, near, far, query, keep, send, after):
    rows, width = query.shape
    operands, specs = [], []
    for x in (near, far):
        for part in (half_rows(x, frames, mine, 1), half_rows(x, frames, mine, 0)):
            operands.append(part[0])
            specs.append(part[1])
    grad = pl.BlockSpec((1, *keep.shape[1:]), lambda i, c: (jnp.maximum(i - 1, 0), 0, 0, 0))
    out = pl.BlockSpec((width // 2, width), lambda i, c: (0, i))
    return call(
        attend_grads_kernel,
        "attend_grads",
        [shape(width // 2, width)] * 3 + [shape(width // 2, 3 * width)],
        [*specs, whole(query), grad, grad],
        [pl.BlockSpec((width // 2, width), lambda i, c: (0, 0))] * 3 + [out],
        grid=(3,),
        scalars=1,
        after=after,
    )(mine, *operands, query, keep, send)


def embed_back_kernel(side_ref, *refs):
    halves, (fields_ref, send_ref, keep_ref, own_send_ref, own_keep_ref, lead_ref, turned) = refs[:4], refs[4:]
    half, rows = halves[0].shape
    own = own_send_ref.shape[1]

    @pl.when(pl.program_id(0) == 0)
    def _():
        for i in range(2):

            @pl.when(side_ref[1] ^ i == side_ref[2])
            def _(i=i):
                place = pl.multiple_of(side_ref[1] * own, 128)
                own_send_ref[...] = halves[2 * i][:, pl.ds(place, own)]
                own_keep_ref[...] = halves[2 * i + 1][:, pl.ds(place, own)]

            turned[i] = jnp.concatenate([halves[2 * i][...], halves[2 * i + 1][...]], axis=0).T
        lead = jnp.sum(turned[0].astype(F32), axis=0, keepdims=True)
        lead = lead + jnp.sum(turned[1].astype(F32), axis=0, keepdims=True)
        lead_ref[...] = jnp.broadcast_to(lead, lead_ref.shape)

    x = None
    for i in range(2):
        place = pl.multiple_of((side_ref[1] ^ i) * rows, 128)
        part = dot(fields_ref[:, pl.ds(place, rows)], turned[i], 1, 0)
        x = part if x is None else x + part
    x = x.astype(BF).T
    send_ref[...] = x[:half]
    keep_ref[...] = x[half:]


def embed_back(sides, got, fields, own, after):
    rows = got[0].shape[1]
    half = got[0].shape[0] // 32 * 16
    lines, patches = fields.shape
    block = max(b for b in (1152, 576, 384, 128) if lines % b == 0)
    operands = [x for x in got for _ in range(2)]
    specs = [
        pl.BlockSpec((half, rows), lambda i, c, flip=flip: (c[0] ^ flip, 0)) for _ in got for flip in (1, 0)
    ]
    out = pl.BlockSpec((half, block), lambda i, c: (0, i))
    out_shape = [shape(half, lines)] * 2 + [shape(half, own)] * 2 + [shape(8, 2 * half, kind=F32)]
    return call(
        embed_back_kernel,
        "embed_back",
        out_shape,
        [*specs, pl.BlockSpec((block, patches), lambda i, c: (i, 0))],
        [out, out, *[whole(a) for a in out_shape[2:]]],
        grid=(lines // block,),
        scratch=[pltpu.VMEM((2, rows, 2 * half), BF)],
        scalars=1,
        cost=100,
        after=after,
    )(sides, *operands, fields)


def start_back_kernel(frames, keep_ref, core_ref, chan_ref, start_ref, gain_ref, mid_ref, out_ref):
    rows, width = start_ref.shape
    grad = keep_ref[...] + core_ref[...].astype(F32) + chan_ref[...].astype(F32)
    n, r = norm_parts(start_ref[...])
    start = mid_ref[...] + norm_back(grad, n, r, gain_ref[...])
    turned = start.T
    per = width // frames
    turned = [turned[f * per : (f + 1) * per] for f in (*range(0, frames, 2), *range(1, frames, 2))]
    out_ref[:width, :] = jnp.concatenate(turned, axis=0).astype(BF)
    lines = []
    for x in (grad * n, grad):
        x = jnp.sum(x, axis=0, keepdims=True)
        lines += [x[:, j : j + rows] for j in range(0, width, rows)]
    lines.append(jnp.zeros((16 - len(lines), rows), F32))
    out_ref[width:, :] = jnp.concatenate(lines, axis=0).astype(BF)


def start_back(frames, keep, core, far, start, gain, mid_grad, after):
    rows, width = start.shape
    operands = [keep, core, far, start, gain[None], mid_grad]
    out_shape = shape(width + 16, rows)
    return call(
        partial(start_back_kernel, frames),
        "start_back",
        out_shape,
        [pl.BlockSpec((rows, width), lambda i: (0, 0))] * 2 + [whole(a) for a in operands[2:]],
        whole(out_shape),
        grid=(1,),
        cost=100,
        after=after,
    )(*operands)


def pull_kernel(chunk_ref, fields_ref, cot_ref, offset_ref, *rest):
    chunk, step = pl.program_id(0), pl.program_id(1)
    outs, total = rest[:-1], rest[-1]

    @pl.when(step == 0)
    def _():
        total[...] = jnp.zeros_like(total)

    high = 16
    for i in range(0, PIX, high):
        lines = slice(i, i + high)
        sums = [total[e * PIX + i : e * PIX + i + high, :] for e in range(EXP - 1)]
        for c in range(cot_ref.shape[0]):
            g = cot_ref[c, lines, :].astype(F32)
            first = fields_ref[0, c, lines, :].astype(F32)
            shift = offset_ref[0, c, lines, :]
            for e in range(EXP - 1):
                x = fields_ref[e + 1, c, lines, :].astype(F32) - first
                sums[e] = sums[e] + g * (x + (offset_ref[e + 1, c, lines, :] - shift))
        for e in range(EXP - 1):
            total[e * PIX + i : e * PIX + i + high, :] = sums[e]

    for s, out_ref in enumerate(outs):

        @pl.when((step == pl.num_programs(1) - 1) & (chunk == s))
        def _(out_ref=out_ref):
            out_ref[...] = total[...].astype(BF)


def pull(numbers, fields, cot, offset):
    chan = numbers.shape[0]
    channels, pixels, patches = cot.shape
    rows = patches // chan
    block = max(b for b in (6, 3, 2, 1) if channels % b == 0)
    high = (EXP - 1) * PIX
    return call(
        pull_kernel,
        "pull",
        [shape(high, rows)] * chan,
        [
            pl.BlockSpec((EXP, block, PIX, rows), lambda s, i, r: (0, i, 0, r[s])),
            pl.BlockSpec((block, PIX, rows), lambda s, i, r: (i, 0, r[s])),
            pl.BlockSpec((EXP, block, PIX, 1), lambda s, i, r: (0, i, 0, 0)),
        ],
        [pl.BlockSpec((high, rows), lambda s, i, r: (0, 0))] * chan,
        grid=(chan, channels // block),
        scratch=[pltpu.VMEM((high, rows), F32)],
        scalars=1,
    )(numbers, fields, cot, offset)


def blend_kernel(chunk_ref, *refs):
    gate_refs, (fields_ref, cot_ref, offset_ref, mixed_ref, bias_ref, gates_ref) = refs[:2], refs[2:]
    channels, _, patches = cot_ref.shape
    wide, rows = EXP * PIX, gate_refs[0].shape[1]

    @pl.when(pl.program_id(0) == 0)
    def _():
        for i, gate_ref in enumerate(gate_refs):
            place = pl.multiple_of((chunk_ref[0] ^ i) * rows, 128)
            gates_ref[:, pl.ds(place, rows)] = gate_ref[:wide, :]

    high, across = 16, 384
    for i in range(0, PIX, high):
        lines = slice(i, i + high)
        for j in range(0, patches, across):
            cols = slice(j, j + across)
            gates = [gates_ref[e * PIX + i : e * PIX + i + high, cols].astype(F32) for e in range(EXP)]
            for c in range(channels):
                mixed = None
                for e in range(EXP):
                    x = fields_ref[e, c, lines, cols].astype(F32) + offset_ref[e, c, lines, :]
                    term = gates[e] * x
                    mixed = term if mixed is None else mixed + term
                mixed_ref[c, lines, cols] = mixed.astype(BF)
    here = lax.broadcasted_iota(jnp.int32, (PIX, wide), 0)
    there = lax.broadcasted_iota(jnp.int32, (PIX, wide), 1) % PIX
    x = dot(cot_ref[...].reshape(channels * PIX, patches), gates_ref[...], 1, 1)
    for c in range(channels):
        part = jnp.where(here == there, x[c * PIX : (c + 1) * PIX], 0.0)
        bias_ref[0, c : c + 1, :] = jnp.sum(part, axis=0, keepdims=True)


def blend(chunk, gates, fields, cot, offset, after):
    channels, pixels, patches = cot.shape
    block = max(b for b in (6, 3, 2, 1) if channels % b == 0)
    steps = channels // block
    out_shape = [shape(*cot.shape), shape(steps, block, EXP * PIX, kind=F32), shape(EXP * PIX, patches)]
    return call(
        blend_kernel,
        "blend",
        out_shape,
        [
            *[whole(a) for a in gates],
            pl.BlockSpec((EXP, block, PIX, patches), lambda i, c: (0, i, 0, 0)),
            pl.BlockSpec((block, PIX, patches), lambda i, c: (i, 0, 0)),
            pl.BlockSpec((EXP, block, PIX, 1), lambda i, c: (0, i, 0, 0)),
        ],
        [
            pl.BlockSpec((block, PIX, patches), lambda i, c: (i, 0, 0)),
            pl.BlockSpec((1, block, EXP * PIX), lambda i, c: (i, 0, 0)),
            whole(out_shape[2]),
        ],
        grid=(steps,),
        scalars=1,
        after=after,
    )(chunk, *gates, fields, cot, offset)


def fields_back_kernel(frames, chunk_ref, weight_ref, turned_ref, gate_ref, cot_ref, *rest):
    out_ref, start = rest[-2:]
    width = weight_ref.shape[2]
    per = width // frames

    @pl.when(pl.program_id(0) == 0)
    def _():
        x = turned_ref[:width, :].astype(F32)
        order = [(f % 2) * (frames // 2) + f // 2 for f in range(frames)]
        start[...] = jnp.concatenate([x[g * per : (g + 1) * per] for g in order], axis=0).astype(BF)

    grad = dot(weight_ref[0], start[...], 1, 0)
    gate = gate_ref[...].astype(F32)
    for c in range(cot_ref.shape[0]):
        lines = slice(c * PIX, (c + 1) * PIX)
        out_ref[0, lines, :] = (grad[lines, :] + gate * cot_ref[c].astype(F32)).astype(BF)


def fields_back(frames, chunk, weight, turned, gates, cot, grad, after):
    channels, pixels, patches = cot.shape
    rows = turned.shape[1]
    width = weight.shape[2]
    in_specs = [
        pl.BlockSpec((1, channels * PIX, width), lambda e, r: (e, 0, 0)),
        whole(turned),
        pl.BlockSpec((PIX, rows), lambda e, r: (e, r[0])),
        pl.BlockSpec((channels, PIX, rows), lambda e, r: (0, 0, r[0])),
    ]
    operands = [chunk, weight, turned, gates, cot]
    more = {}
    if grad is not None:
        in_specs.append(pl.BlockSpec(memory_space=pl.ANY))
        operands.append(grad)
        more = {"input_output_aliases": {5: 0}}
    return call(
        partial(fields_back_kernel, frames),
        "fields_back",
        shape(EXP, channels * PIX, patches),
        in_specs,
        pl.BlockSpec((1, channels * PIX, rows), lambda e, r: (e, 0, r[0])),
        grid=(EXP,),
        scratch=[pltpu.VMEM((width, rows), BF)],
        scalars=1,
        after=after,
        **more,
    )(*operands)


def norm_parts(v):
    centred = v - jnp.mean(v, axis=-1, keepdims=True)
    spread = jnp.mean(centred * centred, axis=-1, keepdims=True)
    r = lax.rsqrt(spread + epsilon)
    return centred * r, r


def norm_back(grad, n, r, gain):
    t = grad * gain
    return r * (
        t - jnp.mean(t, axis=-1, keepdims=True) - n * jnp.mean(t * n, axis=-1, keepdims=True)
    )


def add_low(a, b):
    return (a.astype(F32) + b.astype(F32)).astype(BF)


def halve(x, axis, mine):
    keep = lax.dynamic_index_in_dim(x, mine, axis, keepdims=False)
    send = lax.dynamic_index_in_dim(x, 1 - mine, axis, keepdims=False)
    return keep, send


def merge_kernel(blocks, side_ref, *refs):
    ins, (send_ref, keep_ref) = refs[:-2], refs[-2:]

    def put(gone, gone_far, kept, kept_far):
        for a, b, out_ref in ((gone, gone_far, send_ref), (kept, kept_far, keep_ref)):
            x = a[...].astype(F32) + b[...].astype(F32)
            out_ref[...] = x.astype(BF).reshape(out_ref.shape)

    if blocks == 0:
        (gone, kept), n = ins[:2], len(ins) // 2 - 1
        for i in range(n):
            far = ins[2 + i], ins[2 + n + i]
            pl.when(pl.program_id(0) == i)(lambda far=far: put(gone, far[0], kept, far[1]))
    elif len(ins) == 4:
        put(*ins)
    else:
        pl.when(pl.program_id(0) < blocks)(lambda: put(*ins[:4]))
        pl.when(pl.program_id(0) == blocks)(lambda: put(*ins[4:]))


def merge(keep, far, side, window, more, cost, after):
    a, _, rows, n = keep.shape
    first, count = window or (0, n)
    if isinstance(far, list):
        return merge_parts(keep, far, side, after)
    block = more[0].shape[3] if more else max(
        b for b in (1024, 768, 640, 384, 256, 128) if count % b == 0 and first % b == 0 and (b < count or b < 512)
    )
    blocks = count // block
    specs = [
        pl.BlockSpec(
            (a, 1, rows, block),
            lambda i, c, flip=flip: (0, c[0] ^ flip, 0, jnp.minimum(i, blocks - 1) + first // block),
        )
        for flip in (1, 1, 0, 0)
    ]
    operands = [keep, far, keep, far]
    if more:
        specs += [
            pl.BlockSpec((a, 1, rows, block), lambda i, c, flip=flip: (0, c[0] ^ flip, 0, 0))
            for flip in (1, 1, 0, 0)
        ]
        operands += [*more, *more]
    steps = blocks + (1 if more else 0)
    out = pl.BlockSpec((a, rows, block), lambda i, c: (0, 0, i))
    return call(
        partial(merge_kernel, blocks),
        "merge",
        [shape(a, rows, steps * block)] * 2,
        specs,
        [out, out],
        grid=(steps,),
        scalars=1,
        cost=cost,
        after=after,
    )(side.astype(jnp.int32)[None], *operands)


def merge_parts(keep, far, side, after):
    a, _, rows, n = keep.shape
    block = n // len(far)

    def spec(flip, step):
        return pl.BlockSpec((a, 1, rows, block), lambda i, c: (0, c[0] ^ flip, 0, i * step))

    out = pl.BlockSpec((a, rows, block), lambda i, c: (0, 0, i))
    return call(
        partial(merge_kernel, 0),
        "merge",
        [shape(a, rows, n)] * 2,
        [spec(1, 1), spec(0, 1), *[spec(1, 0) for _ in far], *[spec(0, 0) for _ in far]],
        [out, out],
        grid=(len(far),),
        scalars=1,
        after=after,
    )(side.astype(jnp.int32)[None], keep, keep, *far, *far)


class Sum:
    def __init__(self, plan, f, z, order, keep, far, window=None, more=None):
        self.plan, self.at, self.order = plan, {"f": f, "z": z}, list(order)
        self.left = sorted(order, key=lambda b: (b[0] != "f", -b[1]))
        self.keep, self.far, self.window, self.more = keep, far, window, more

    def step(self, after, cost=0):
        axis, bit = self.order.pop(0)
        a = 2 ** self.left.index((axis, bit))
        def rows(x):
            return [rows(y) for y in x] if isinstance(x, list) else x.reshape(a, 2, -1, x.shape[-1])

        keep, far, *more = (rows(x) for x in (self.keep, self.far, *(self.more or ())))
        side = (self.at[axis] // bit) % 2
        send, self.keep = merge(keep, far, side, self.window, more, cost, after)
        self.far = (self.plan.swap_frame if axis == "f" else self.plan.swap_chan)(send, bit)
        self.window = self.more = None
        self.left.remove((axis, bit))
        return send

    def finish(self):
        while self.order:
            self.step([])
        n = self.keep.shape[-1]
        return self.keep.reshape(-1, n).astype(F32) + self.far.reshape(-1, n).astype(F32)


def on_device(
    plan,
    fields,
    lead_index,
    embed_weight,
    position_embed,
    lead_table,
    attend_gain,
    attend_shift,
    attend_weight,
    out_weight,
    out_bias,
    mixer_gain,
    mixer_shift,
    up_weight,
    up_bias,
    down_weight,
    down_bias,
    head_weight,
    specialist_cell_offset,
    cotangent,
):
    f, z = lax.axis_index("frames"), lax.axis_index("chan")
    chan, frames = plan.chan, plan.frames
    width = attend_gain.shape[0]
    hidden_width = up_bias.shape[0]
    channels, pixels, patches = cotangent.shape[1:]
    rows = position_embed.shape[0]
    lines = EXP * channels * PIX
    own_fields, cot = fields[0], cotangent[0]
    flat_fields = own_fields.reshape(lines, patches)
    flat_weight = embed_weight.reshape(lines, width)
    offset = specialist_cell_offset[..., None]
    numbers = jnp.stack([z ^ s for s in range(chan)]).astype(jnp.int32)
    mine = (f % 2).astype(jnp.int32)[None]

    onehot = (
        lead_index[:, None] == jnp.arange(lead_table.shape[0], dtype=jnp.int32)[None, :]
    ).astype(BF)
    lead_vector = dot(onehot, lead_table, 1, 0)
    got = []
    for s in reversed(range(chan)):
        block = lax.dynamic_slice(flat_fields, (0, (z ^ s) * rows), (lines, rows))
        part = dot(block, flat_weight, 0, 0)
        if s == 0:
            part = part + position_embed.astype(F32) + lead_vector
        got.append(plan.to_worker(part.astype(BF), s))

    def flag(x):
        return x.astype(jnp.int32)[None]

    core, low = f % 2, z % 2

    pulls = pull(numbers, own_fields, cot, offset)
    vectors = jnp.concatenate([out_bias, mixer_gain, mixer_shift, down_bias, up_bias])[None]

    stream_start, normed = first_norm(got, attend_gain, attend_shift, [pulls[0], vectors])
    normed_chan = plan.swap_chan(normed, 1)
    near, near_turned, queries = project(normed, plan.swap_frame(normed, 1), attend_weight, True, [])
    pulls = [plan.to_worker(a, s) for s, a in enumerate(pulls)]
    (normed_chan,) = relay([normed_chan], [near])
    far, far_turned = project(normed_chan, plan.swap_frame(normed_chan, 1), attend_weight, False, [])
    attended, attended_turned, shares, rinv = attend(queries, near, far)

    (
        gate, _, mid_grad, attended_low, normed_turned, end_turned, down_low, logit_low, branch_low,
        active_turned, hidden_low,
    ) = middle(stream_start, attended, out_weight, vectors, head_weight, pulls, up_weight, down_weight)

    gate = plan.from_workers(beside(flag(core), gate, plan.swap_frame(gate, 1), []))

    query_low, keep_grad, send_grad = attend_back(queries, near, far, attended, attended_low, shares, rinv, [])
    send = project_back(send_grad, attend_weight, gate)
    keep = project_back(keep_grad, attend_weight, [send], query_low)
    send = plan.swap_frame(send, 1)
    far_grad = (keep[rows:] + send[rows:].astype(F32)).astype(BF)
    going = [far_grad]
    far_grad = plan.swap_chan(far_grad, 1)

    n_wide = hidden_width + (-hidden_width % WIDE) + WIDE
    weights = tall_grads(frames, chan, active_turned, down_low, n_wide, going)
    weights = wide_grads(normed_turned, hidden_low, attended_turned, branch_low, end_turned, logit_low, weights)
    step = weights
    weights = lax.psum_scatter(weights, "frames", scatter_dimension=0, tiled=True)

    sent = start_back(frames, keep, send, far_grad, stream_start, attend_gain, mid_grad, [step])
    sent = beside(flag(core), sent, plan.swap_frame(sent, 1), [])
    got = plan.from_workers(sent)

    *attend_send, attend_keep = attend_grads(
        frames, mine, near_turned, far_turned, query_low, keep_grad, send_grad, [sent]
    )
    high = [("f", bit) for bit in bits_of(frames)[1:]]
    lower = [("z", bit) for bit in bits_of(chan)]
    projections = Sum(plan, f, z, high + lower, attend_keep, [plan.swap_frame(a, 1) for a in attend_send])

    mixed, expert_bias, gates = blend(flag(low), gate, own_fields, cot, offset, attend_send)

    step = projections.step([mixed])
    sides = jnp.concatenate([mine, flag(low), flag(z // plan.half)])
    embed_send, embed_keep, own_send, own_keep, lead = embed_back(sides, got, flat_fields, rows, [step])
    embed_far, own_far = plan.swap_frame(embed_send, 1), plan.swap_frame(own_send, 1)
    cut = (lines // rows + 1) // 2 * rows
    embed_sums = [
        Sum(plan, f, z, high, embed_keep, embed_far, (0, cut)),
        Sum(plan, f, z, high[::-1], embed_keep, embed_far, (cut, lines - cut), (own_keep, own_far)),
    ]
    step = projections.step([embed_send], 30)
    step = embed_sums[0].step([step])
    step = embed_sums[1].step([step])
    (weights,) = relay([weights], [step])
    step = weights
    weights = lax.psum_scatter(weights, "chan", scatter_dimension=0, tiled=True)
    wide_weight = embed_weight.reshape(EXP, channels * PIX, width)
    fields_grad = fields_back(frames, flag(low), wide_weight, got[0], gates, cot, None, [step])

    per = width // frames
    lead = lead[0].reshape(2, frames // 2, per)
    lead = jnp.swapaxes(jnp.where(core == 0, lead[::-1], lead), 0, 1).reshape(-1, rows)
    own = (jnp.arange(frames) == f).astype(F32)
    n_lead = lead.shape[0]
    parts = [
        sum(a[EXP * PIX :, i : i + rows].astype(F32) for a in gate for i in (0, rows)),
        sum(a[width : width + 2 * n_lead, i : i + rows].astype(F32) for a in got for i in (0, rows)),
        (own[:, None, None] * lead).reshape(-1, rows),
        jnp.pad(own * lead_index.astype(F32), (0, rows - frames))[None],
        expert_bias.reshape(-1, rows),
    ]
    small = jnp.concatenate(parts, axis=0)
    (small,) = relay([jnp.pad(small, ((0, -small.shape[0] % 16), (0, 0))).astype(BF)], [fields_grad])
    others = iter(bits_of(frames))
    small_far = plan.swap_frame(small, next(others))
    fields_grad = fields_back(frames, flag(1 - low), wide_weight, got[1], gates, cot, fields_grad, [small])
    step = projections.step([fields_grad])
    step = embed_sums[0].step([step]) if embed_sums[0].order else step
    step = embed_sums[1].step([step, weights]) if embed_sums[1].order else step
    step = projections.step([step])
    for i, bit in enumerate(others):
        small = plus(small, small_far, [step])
        small_far = plan.swap_frame(small, bit)
        step = small

    weights = weights.astype(F32)
    small = small.astype(F32) + small_far.astype(F32)
    cuts, first = [], 0
    for a in parts:
        cuts.append(small[first : first + a.shape[0]])
        first += a.shape[0]
    vectors, norms, lead, index, bias = cuts
    here = f * chan + z
    n_each = width // (frames * chan)

    def own_part(x, n=n_each, axis=0):
        return lax.dynamic_slice_in_dim(x, here * n, n, axis)

    vectors_out = jnp.concatenate([vectors[: 4 * n_lead], norms], axis=0).reshape(6, width)
    vectors_out = own_part(vectors_out, axis=1)
    up_bias_out = own_part(vectors[4 * n_lead :].reshape(-1), hidden_width // (frames * chan))
    rows_of_table = index[0, :frames, None] == jnp.arange(lead_table.shape[0], dtype=F32)[None]
    lead = own_part(lead.reshape(frames, width), axis=1)
    table_out = jnp.sum(rows_of_table[:, :, None].astype(F32) * lead[:, None, :], axis=0)
    bias = lax.dynamic_slice_in_dim(bias.reshape(channels, EXP, PIX), f * (PIX // frames), PIX // frames, 2)
    bias_out = jnp.swapaxes(bias, 0, 1)
    first, second = (a.finish() for a in embed_sums)
    n = lines - first.shape[1]
    embed_out = jnp.concatenate([first, second[:, :n]], axis=1).T.reshape(EXP, channels, PIX, per)
    position_out = second[:, n:].T
    attend_out = projections.finish()
    tall = weights[:, :hidden_width].reshape(n_each, -1, width)
    tall = jnp.swapaxes(tall, 0, 1).reshape(-1, width)
    wide = weights[:, hidden_width:]

    return (
        mixed[None],
        fields_grad.reshape(fields.shape),
        embed_out,
        position_out,
        table_out,
        vectors_out[4],
        vectors_out[5],
        attend_out,
        wide[:, hidden_width : hidden_width + width],
        vectors_out[2],
        vectors_out[0],
        vectors_out[1],
        wide[:, :hidden_width],
        up_bias_out,
        tall,
        vectors_out[3],
        wide[:, hidden_width + width : hidden_width + width + EXP * PIX],
        bias_out,
    )


def solution(mesh):
    plan = Plan(mesh.shape["frames"], mesh.shape["chan"])
    both = ("frames", "chan")
    in_specs = (
        P("frames", None, "chan", None, None),
        P("frames"),
        P(None, "chan", None, None),
        P("chan", None),
        *[P()] * 13,
        P(None, "chan", None),
        P("frames", "chan", None, None),
    )
    out_specs = (
        P("frames", "chan", None, None),
        P("frames", None, "chan", None, None),
        P(None, "chan", None, "frames"),
        P("chan", "frames"),
        P(None, both),
        P(both),
        P(both),
        P(both, None),
        P(both, None),
        P(both),
        P(both),
        P(both),
        P(both, None),
        P(both),
        P(both, None),
        P(both),
        P(both, None),
        P(None, "chan", "frames"),
    )
    return jax.shard_map(
        partial(on_device, plan), mesh=mesh, in_specs=in_specs, out_specs=out_specs, check_vma=False
    )
```

```python
from functools import partial

import jax
import jax.numpy as jnp
from jax import lax
from jax.experimental import pallas as pl
from jax.experimental.pallas import tpu as pltpu
from jax.sharding import PartitionSpec as P

HEADS = 12
HEAD_DIM = 64
EXP = 3
PIX = 64
LOG2E = 1.4426950408889634

epsilon = 1e-05
BF = jnp.bfloat16
F32 = jnp.float32


def dot(left, right, left_dim, right_dim):
    return lax.dot_general(
        left, right, (((left_dim,), (right_dim,)), ((), ())), preferred_element_type=F32
    )


class Plan:
    def __init__(self, frames, chan):
        self.frames, self.chan, self.half = frames, chan, chan // 2

    def pairs(self, target):
        return [
            (f * self.chan + z, (lambda t: t[0] * self.chan + t[1])(target(f, z)))
            for f in range(self.frames)
            for z in range(self.chan)
        ]

    def swap_frame(self, x, bit):
        return lax.ppermute(x, ("frames", "chan"), self.pairs(lambda f, z: (f ^ bit, z)))

    def swap_chan(self, x, bit):
        return lax.ppermute(x, ("frames", "chan"), self.pairs(lambda f, z: (f, z ^ bit)))

    def worker(self, f, r):
        return (f & ~1) + r % 2, (f & 1) * self.half + r // 2

    def to_worker(self, x, s):
        return lax.ppermute(
            x, ("frames", "chan"), self.pairs(lambda f, z: self.worker(f, z ^ s))
        )

    def from_workers(self, pair):
        return [
            lax.ppermute(x, ("frames", "chan"), self.sources(lambda f, z: self.holder(f, z, i)))
            for i, x in enumerate((pair, pair))
        ]

    def holder(self, f, z, i):
        return (f & ~1) + z // self.half, (f & 1) * self.half + (z + i) % self.half

    def sources(self, source):
        return [(a, b) for b, a in self.pairs(source)]


def bits_of(n):
    return [1 << i for i in range(n.bit_length() - 1)]


VMEM = 52 << 20


def call(kernel, name, out_shape, in_specs, out_specs, grid=(), scratch=(), scalars=0, cost=0, after=(), **more):
    n_in = scalars + len(in_specs)

    def body(*refs):
        kernel(*refs[:n_in], *refs[n_in + len(after) :])

    run = pl.pallas_call(
        body,
        grid_spec=pltpu.PrefetchScalarGridSpec(
            num_scalar_prefetch=scalars,
            grid=grid,
            in_specs=[*in_specs, *[pl.BlockSpec(memory_space=pl.ANY) for _ in after]],
            out_specs=out_specs,
            scratch_shapes=scratch,
        ),
        out_shape=out_shape,
        compiler_params=pltpu.CompilerParams(vmem_limit_bytes=VMEM),
        cost_estimate=pl.CostEstimate(flops=1 + cost * 10**9, bytes_accessed=1, transcendentals=0),
        name=name,
        **more,
    )
    return lambda *operands: run(*operands, *after)


def shape(*dims, kind=BF):
    return jax.ShapeDtypeStruct(dims, kind)


def whole(x):
    return pl.BlockSpec(x.shape, lambda *_: (0,) * len(x.shape))


def first_norm_kernel(a_ref, b_ref, c_ref, d_ref, gain_ref, shift_ref, start_ref, normed_ref):
    start = sum(x[...].astype(F32) for x in (a_ref, b_ref, c_ref, d_ref))
    start_ref[...] = start
    n, _ = norm_parts(start)
    normed_ref[...] = (n * gain_ref[...] + shift_ref[...]).astype(BF)


def first_norm(parts, gain, shift, after):
    rows, width = parts[0].shape
    operands = [*parts, gain[None], shift[None]]
    out_shape = [shape(rows, width, kind=F32), shape(rows, width)]
    return call(
        first_norm_kernel,
        "first_norm",
        out_shape,
        [whole(a) for a in operands],
        [whole(a) for a in out_shape],
        after=after,
    )(*operands)


def project_kernel(first, near_ref, far_ref, weight_ref, kv_ref, turned_ref, *rest):
    rows = near_ref.shape[0]
    pairs, _, lanes = kv_ref.shape
    step = pl.program_id(0)

    def put():
        for i, x_ref in enumerate((near_ref, far_ref)):
            x = dot(x_ref[...], weight_ref[...], 1, 0).astype(BF)
            for p in range(pairs):
                kv_ref[p, i * rows : (i + 1) * rows, :] = x[:, p * lanes : (p + 1) * lanes]

    @pl.when(step == 0)
    def _():
        for i, x_ref in enumerate((near_ref, far_ref)):
            turned_ref[:, i * rows : (i + 1) * rows] = x_ref[...].T

    if first:

        @pl.when(step == 0)
        def _():
            rest[0][...] = dot(near_ref[...], weight_ref[...], 1, 0).astype(BF)

        pl.when(step > 0)(put)
    else:
        put()


def project(near, far, weight, first, after):
    rows, width = near.shape
    pair = 2 * HEAD_DIM
    pairs = width // pair
    skip = 0 if first else 1
    out_shape = [shape(2 * pairs, 2 * rows, pair), shape(width, 2 * rows)]
    out_specs = [
        pl.BlockSpec((pairs, 2 * rows, pair), lambda i: (jnp.maximum(i + skip - 1, 0), 0, 0)),
        whole(out_shape[1]),
    ]
    if first:
        out_shape.append(shape(rows, width))
        out_specs.append(whole(out_shape[2]))
    return call(
        partial(project_kernel, first),
        "project",
        out_shape,
        [whole(near), whole(far), pl.BlockSpec((width, width), lambda i: (0, i + skip))],
        out_specs,
        grid=(3 - skip,),
        after=after,
    )(near, far, weight)


def attend_kernel(
    q_ref, near_ref, far_ref, near_value_ref, far_value_ref, o_ref, turned_ref, e_ref, rinv_ref
):
    scale = HEAD_DIM ** (-0.5) * LOG2E
    lanes = q_ref.shape[1]
    for h in range(lanes // HEAD_DIM):
        cols = slice(h * HEAD_DIM, (h + 1) * HEAD_DIM)
        q = q_ref[:, cols]
        s_near = dot(q, near_ref[0, :, cols], 1, 1)
        s_far = dot(q, far_ref[0, :, cols], 1, 1)
        m = jnp.maximum(
            jnp.max(s_near, axis=1, keepdims=True), jnp.max(s_far, axis=1, keepdims=True)
        )
        e_near = jnp.exp2((s_near - m) * scale)
        e_far = jnp.exp2((s_far - m) * scale)
        total = jnp.sum(e_near, axis=1, keepdims=True) + jnp.sum(e_far, axis=1, keepdims=True)
        e_near, e_far = e_near.astype(BF), e_far.astype(BF)
        keys = e_near.shape[1]
        e_ref[h, :, :keys] = e_near
        e_ref[h, :, keys:] = e_far
        o = dot(e_near, near_value_ref[0, :, cols], 1, 0) + dot(e_far, far_value_ref[0, :, cols], 1, 0)
        rinv = jnp.broadcast_to(1.0 / total, o.shape)
        rinv_ref[:, cols] = rinv
        o_ref[:, cols] = (o * rinv).astype(BF)
    turned_ref[...] = o_ref[...].T


def attend(q, near, far):
    rows, width = q.shape
    keys = near.shape[1]
    lanes = 2 * HEAD_DIM
    steps = width // lanes
    row_spec = pl.BlockSpec((rows, lanes), lambda i: (0, i))
    key_spec = pl.BlockSpec((1, keys, lanes), lambda i: (i, 0, 0))
    value_spec = pl.BlockSpec((1, keys, lanes), lambda i: (i + steps, 0, 0))
    e_spec = pl.BlockSpec((2, rows, 2 * keys), lambda i: (i, 0, 0))
    return call(
        attend_kernel,
        "attend",
        [
            shape(rows, width),
            shape(width, rows),
            shape(HEADS, rows, 2 * keys),
            shape(rows, width, kind=F32),
        ],
        [row_spec, key_spec, key_spec, value_spec, value_spec],
        [row_spec, pl.BlockSpec((lanes, rows), lambda i: (i, 0)), e_spec, row_spec],
        grid=(steps,),
    )(q, near, far, near, far)


def attend_back_kernel(
    q_ref, near_ref, far_ref, near_value_ref, far_value_ref, o_ref, do_ref, e_ref, rinv_ref,
    dq_ref, keep_ref, send_ref,
):
    scale = HEAD_DIM ** (-0.5)
    rows, lanes = q_ref.shape
    for h in range(lanes // HEAD_DIM):
        cols = slice(h * HEAD_DIM, (h + 1) * HEAD_DIM)
        q = q_ref[:, cols]
        do = do_ref[:, cols].astype(F32) * rinv_ref[:, cols]
        inner = jnp.sum(do * o_ref[:, cols].astype(F32), axis=1, keepdims=True)
        do = do.astype(BF)
        dq = None
        for i, (k_ref, v_ref) in enumerate(((near_ref, near_value_ref), (far_ref, far_value_ref))):
            keys = k_ref.shape[1]
            e = e_ref[h, :, i * keys : (i + 1) * keys]
            dp = dot(do, v_ref[0, :, cols], 1, 1)
            ds = (e.astype(F32) * (dp - inner)).astype(BF)
            part = dot(ds, k_ref[0, :, cols], 1, 0)
            dq = part if dq is None else dq + part
            dk = (dot(ds, q, 0, 0) * scale).astype(BF)
            dv = dot(e, do, 0, 0).astype(BF)
            lines = slice(i * rows, (i + 1) * rows)
            for k, x in enumerate((dk, dv)):
                keep_ref[k, 0, lines, cols] = x[:rows]
                send_ref[k, 0, lines, cols] = x[rows:]
        dq_ref[:, cols] = (dq * scale).astype(BF)


def attend_back(q, near, far, o, do, e, rinv, after):
    rows, width = q.shape
    keys = near.shape[1]
    lanes = 2 * HEAD_DIM
    steps = width // lanes
    row_spec = pl.BlockSpec((rows, lanes), lambda i: (0, i))
    key_spec = pl.BlockSpec((1, keys, lanes), lambda i: (i, 0, 0))
    value_spec = pl.BlockSpec((1, keys, lanes), lambda i: (i + steps, 0, 0))
    e_spec = pl.BlockSpec((2, rows, 2 * keys), lambda i: (i, 0, 0))
    return call(
        attend_back_kernel,
        "attend_back",
        [shape(rows, width), *[shape(2, steps, keys, lanes)] * 2],
        [row_spec, key_spec, key_spec, value_spec, value_spec, row_spec, row_spec, e_spec, row_spec],
        [row_spec, *[pl.BlockSpec((2, 1, keys, lanes), lambda i: (0, i, 0, 0))] * 2],
        grid=(steps,),
        after=after,
    )(q, near, far, near, far, o, do, e, rinv)


def all_pairs(ref, k):
    return jnp.concatenate([ref[k, p] for p in range(ref.shape[1])], axis=1)


def project_back_kernel(grad_ref, weight_ref, *rest):
    step, out_ref = pl.program_id(0), rest[-1]

    @pl.when(step < 2)
    def _():
        x = dot(all_pairs(grad_ref, 0), weight_ref[...], 1, 1)

        @pl.when(step == 0)
        def _():
            rest[-2][...] = x

        @pl.when(step == 1)
        def _():
            out_ref[...] = (rest[-2][...] + x).astype(out_ref.dtype)

    if len(rest) > 2:

        @pl.when(step == 2)
        def _():
            rows = rest[0].shape[0]
            out_ref[:rows, :] += dot(rest[0][...], weight_ref[...], 1, 1)


def project_back(grads, weight, after, *queries):
    _, pairs, rows, lanes = grads.shape
    width = weight.shape[0]
    out_shape = shape(rows, width, kind=F32 if queries else BF)

    def kernel(*refs):
        *ins, out_ref, total = refs
        project_back_kernel(*ins, total, out_ref)

    return call(
        kernel,
        "project_back",
        out_shape,
        [
            pl.BlockSpec((1, pairs, rows, lanes), lambda i: (jnp.minimum(i, 1), 0, 0, 0)),
            pl.BlockSpec((width, width), lambda i: (0, (i + 1) % 3)),
            *[whole(a) for a in queries],
        ],
        whole(out_shape),
        grid=(3 if queries else 2,),
        scratch=[pltpu.VMEM((rows, width), F32)],
        after=after,
    )(grads, weight, *queries)


def relay_kernel(*refs):
    n = len(refs) // 2
    for a, b in zip(refs[:n], refs[n:]):
        b[...] = a[...]


def relay(arrays, after):
    specs = [whole(x) for x in arrays]
    return call(relay_kernel, "relay", [shape(*x.shape) for x in arrays], specs, specs, after=after)(*arrays)


def beside_kernel(core_ref, x_ref, other_ref, out_ref):
    n = x_ref.shape[1]
    for core, (a_ref, b_ref) in enumerate(((x_ref, other_ref), (other_ref, x_ref))):

        @pl.when(core_ref[0] == core)
        def _():
            out_ref[:, :n] = a_ref[...]
            out_ref[:, n:] = b_ref[...]


def beside(core, x, other, after):
    out_shape = shape(x.shape[0], 2 * x.shape[1])
    return call(
        beside_kernel, "beside", out_shape, [whole(x), whole(other)], whole(out_shape), scalars=1, after=after
    )(core, x, other)


def plus_kernel(a_ref, b_ref, out_ref):
    out_ref[...] = (a_ref[...].astype(F32) + b_ref[...].astype(F32)).astype(BF)


def plus(a, b, after):
    return call(plus_kernel, "plus", shape(*a.shape), [whole(a), whole(b)], whole(a), after=after)(a, b)


def middle_kernel(
    start_ref, attended_ref, out_ref, vector_ref, head_ref, pull0_ref, pull1_ref, pull2_ref, pull3_ref, up_any, down_any,
    gate_ref, sum_ref, mid_grad_ref, attended_low_ref, normed_turned_ref, end_turned_ref,
    down_low_ref, logit_low_ref, branch_low_ref, active_any, hidden_any,
    up, down, slope, active_turned, hidden_low, in_sem, out_sem,
):
    rows, width = start_ref.shape
    hidden_width = up.shape[1]
    steps = in_sem.shape[1]
    tile = hidden_width // steps
    tiles = [slice(i * tile, (i + 1) * tile) for i in range(steps)]
    ups = [pltpu.make_async_copy(up_any.at[:, t], up.at[:, t], in_sem.at[0, i]) for i, t in enumerate(tiles)]
    downs = [pltpu.make_async_copy(down_any.at[t], down.at[t], in_sem.at[1, i]) for i, t in enumerate(tiles)]
    outs = [
        pltpu.make_async_copy(active_turned.at[t], active_any.at[t], out_sem.at[0, i])
        for i, t in enumerate(tiles)
    ] + [
        pltpu.make_async_copy(hidden_low.at[:, t], hidden_any.at[:, t], out_sem.at[1, i])
        for i, t in enumerate(tiles)
    ]
    for a, b in zip(ups, downs):
        a.start()
        b.start()
    out_bias, gain, shift, down_bias, up_bias = (
        vector_ref[:, width * i : width * (i + 1) if i < 4 else width * 4 + hidden_width] for i in range(5)
    )
    mid = start_ref[...] + dot(attended_ref[...], out_ref[...], 1, 0) + out_bias
    n, r = norm_parts(mid)
    normed = (n * gain + shift).astype(BF)
    normed_turned_ref[...] = normed.T
    end = mid + down_bias
    k, cube = 0.7978845608028654, 0.044715
    for i, t in enumerate(tiles):
        ups[i].wait()
        h = dot(normed, up[:, t], 1, 0) + up_bias[:, t]
        square = h * h
        th = jnp.tanh(h * (k + (k * cube) * square))
        half = 0.5 + 0.5 * th
        active = (h * half).astype(BF)
        slope[:, t] = half + h * (half * (1.0 - th)) * (k + (3 * k * cube) * square)
        active_turned[t, :] = active.T
        outs[i].start()
        downs[i].wait()
        end = end + dot(active, down[t, :], 1, 0)
    end_low = end.astype(BF)
    end_turned_ref[...] = end_low.T

    logits = dot(end_low, head_ref[...], 1, 0).T
    a, b, c = (logits[e * PIX : (e + 1) * PIX] for e in range(EXP))
    m = jnp.maximum(jnp.maximum(a, b), c)
    a, b, c = jnp.exp(a - m), jnp.exp(b - m), jnp.exp(c - m)
    share = 1.0 / (a + b + c)
    a, b, c = a * share, b * share, c * share
    pull = sum(x[...].astype(F32) for x in (pull0_ref, pull1_ref, pull2_ref, pull3_ref))
    second, third = pull[:PIX], pull[PIX:]
    inner = b * second + c * third
    logit_grad = jnp.concatenate([-a * inner, b * (second - inner), c * (third - inner)], axis=0)
    gate_ref[: EXP * PIX, :] = jnp.concatenate([a, b, c], axis=0).astype(BF)
    logit_low_ref[...] = logit_grad.astype(BF)

    end_grad = dot(logit_grad.T.astype(BF), head_ref[...], 1, 1)
    down_low = end_grad.astype(BF)
    down_low_ref[...] = down_low
    second_grad = jnp.zeros((rows, width), F32)
    per = width // rows
    for i, t in enumerate(tiles):
        grad = dot(down_low, down[t, :], 1, 1) * slope[:, t]
        total = jnp.sum(grad, axis=0, keepdims=True)
        for j in range(tile // rows):
            line = 4 * per + (t.start // rows) + j
            sum_ref[line : line + 1, :] = total[:, j * rows : (j + 1) * rows]
        low = grad.astype(BF)
        hidden_low[:, t] = low
        outs[steps + i].start()
        second_grad = second_grad + dot(low, up[:, t], 1, 1)
    mid_grad = end_grad + norm_back(second_grad, n, r, gain)
    mid_grad_ref[...] = mid_grad
    branch = mid_grad.astype(BF)
    branch_low_ref[...] = branch
    attended_low_ref[...] = dot(branch, out_ref[...], 1, 1).astype(BF)
    for i, x in enumerate((second_grad * n, second_grad, mid_grad, end_grad)):
        x = jnp.sum(x, axis=0, keepdims=True)
        for j in range(per):
            sum_ref[i * per + j : i * per + j + 1, :] = x[:, j * rows : (j + 1) * rows]
    gate_ref[EXP * PIX :, :] = sum_ref[...].astype(BF)
    for a in outs:
        a.wait()


def middle(start, attended, out_w, vectors, head_w, pulls, up_w, down_w):
    rows, width = start.shape
    hidden_width = up_w.shape[1]
    steps = 4
    lines = (4 * width + hidden_width) // rows
    operands = [start, attended, out_w, vectors, head_w, *pulls]
    out_shape = [
        shape(EXP * PIX + lines, rows),
        shape(lines, rows, kind=F32),
        shape(rows, width, kind=F32),
        shape(rows, width),
        shape(width, rows),
        shape(width, rows),
        shape(rows, width),
        shape(EXP * PIX, rows),
        shape(rows, width),
        shape(hidden_width, rows),
        shape(rows, hidden_width),
    ]
    any_spec = pl.BlockSpec(memory_space=pl.ANY)
    return call(
        middle_kernel,
        "middle",
        out_shape,
        [*[whole(a) for a in operands], any_spec, any_spec],
        [*[whole(a) for a in out_shape[:-2]], any_spec, any_spec],
        scratch=[
            pltpu.VMEM((width, hidden_width), BF),
            pltpu.VMEM((hidden_width, width), BF),
            pltpu.VMEM((rows, hidden_width), F32),
            pltpu.VMEM((hidden_width, rows), BF),
            pltpu.VMEM((rows, hidden_width), BF),
            pltpu.SemaphoreType.DMA((2, steps)),
            pltpu.SemaphoreType.DMA((2, steps)),
        ],
    )(*operands, up_w, down_w)


def half_rows(x, blocks, mine, flip):
    per = x.shape[0] // blocks
    x = x.reshape(blocks // 2, 2, per, x.shape[1])
    block = (blocks // 2, 1, per, x.shape[3])
    if per % 16 == 0:
        return x, pl.BlockSpec(block, lambda *a: (0, a[-1][0] ^ flip, 0, 0))
    x = lax.dynamic_index_in_dim(x, mine[0] ^ flip, 1, keepdims=False).reshape(1, 1, -1, x.shape[3])
    return x, whole(x)


def rows_of(ref):
    return ref[...].reshape(-1, ref.shape[3])


def both_halves(send_ref, keep_ref):
    return jnp.concatenate([rows_of(send_ref), rows_of(keep_ref)], axis=0)


def tall_grads_kernel(frames, chan, active_ref, down_ref, out_ref):
    lines, width = active_ref.shape[0], down_ref.shape[1]
    x = dot(active_ref[...], down_ref[...], 1, 0)
    across = out_ref.shape[1] // width
    per = lines // (chan * across * frames)
    parts = [
        jnp.concatenate([x[i + k * per : i + (k + 1) * per] for k in range(across)], axis=1)
        for i in range(0, lines, per * across)
    ]
    out_ref[...] = jnp.concatenate(parts, axis=0).astype(BF)


def tall_grads(frames, chan, active, down, wide, after):
    hidden_width, rows = active.shape
    width = down.shape[1]
    at_once = max(1, frames // 4)
    across = hidden_width // width
    return call(
        partial(tall_grads_kernel, at_once, chan),
        "tall_grads",
        shape(width, hidden_width + wide),
        [pl.BlockSpec((at_once * hidden_width // frames, rows), lambda i: (i, 0)), whole(down)],
        pl.BlockSpec((at_once * width // frames, across * width), lambda i: (i, 0)),
        grid=(frames // at_once,),
        after=after,
    )(active, down)


def wide_grads_kernel(normed_ref, hidden_ref, attended_ref, branch_ref, end_ref, logit_ref, tall_ref, out_ref):
    step, last = pl.program_id(0), pl.num_programs(0) - 1

    @pl.when(step < last)
    def _():
        out_ref[...] = dot(normed_ref[...], hidden_ref[...], 1, 0).astype(BF)

    @pl.when(step == last)
    def _():
        x = dot(attended_ref[...], branch_ref[...], 1, 0)
        y = dot(end_ref[...], logit_ref[...], 1, 1)
        spare = out_ref.shape[1] - x.shape[1] - y.shape[1]
        out_ref[...] = jnp.concatenate([x, y, jnp.zeros((x.shape[0], spare), F32)], axis=1).astype(BF)


WIDE = 1024


def wide_grads(normed, hidden, attended, branch, end, logit, tall):
    width, rows = normed.shape
    hidden_width = hidden.shape[1]
    steps = hidden_width // WIDE + 1
    operands = [normed, hidden, attended, branch, end, logit, tall]
    specs = [whole(x) for x in operands]
    specs[1] = pl.BlockSpec((rows, WIDE), lambda i: (0, jnp.minimum(i, steps - 2)))
    specs[6] = pl.BlockSpec(memory_space=pl.ANY)
    return call(
        wide_grads_kernel,
        "wide_grads",
        shape(*tall.shape),
        specs,
        pl.BlockSpec((width, WIDE), lambda i: (0, i + hidden_width // WIDE)),
        grid=(steps,),
        input_output_aliases={6: 0},
    )(*operands)


def attend_grads_kernel(
    side_ref, near_ref, near2_ref, far_ref, far2_ref, query_ref, keep_grad_ref, send_grad_ref, *rest
):
    sends, keep_ref = rest[:-1], rest[-1]
    rows, width = query_ref.shape
    half = keep_ref.shape[0]
    step = pl.program_id(0)
    near, far = both_halves(near_ref, near2_ref), both_halves(far_ref, far2_ref)

    def put(i, x):
        @pl.when(step == i)
        def _():
            sends[i][...] = x[:half].astype(BF)

        keep_ref[...] = x[half:].astype(BF)

    @pl.when(step == 0)
    def _():
        put(0, dot(near[:, :rows], query_ref[...], 1, 0))

    @pl.when(step > 0)
    def _():
        a, b = all_pairs(keep_grad_ref, 0), all_pairs(send_grad_ref, 0)
        x = dot(near[:, :rows], a[:rows], 1, 0) + dot(near[:, rows:], b[:rows], 1, 0)
        x = x + dot(far[:, :rows], a[rows:], 1, 0) + dot(far[:, rows:], b[rows:], 1, 0)
        put(1, x)
        put(2, x)


def attend_grads(frames, mine, near, far, query, keep, send, after):
    rows, width = query.shape
    operands, specs = [], []
    for x in (near, far):
        for part in (half_rows(x, frames, mine, 1), half_rows(x, frames, mine, 0)):
            operands.append(part[0])
            specs.append(part[1])
    grad = pl.BlockSpec((1, *keep.shape[1:]), lambda i, c: (jnp.maximum(i - 1, 0), 0, 0, 0))
    out = pl.BlockSpec((width // 2, width), lambda i, c: (0, i))
    return call(
        attend_grads_kernel,
        "attend_grads",
        [shape(width // 2, width)] * 3 + [shape(width // 2, 3 * width)],
        [*specs, whole(query), grad, grad],
        [pl.BlockSpec((width // 2, width), lambda i, c: (0, 0))] * 3 + [out],
        grid=(3,),
        scalars=1,
        after=after,
    )(mine, *operands, query, keep, send)


def embed_back_kernel(side_ref, *refs):
    halves, (fields_ref, send_ref, keep_ref, own_send_ref, own_keep_ref, lead_ref, turned) = refs[:4], refs[4:]
    half, rows = halves[0].shape
    own = own_send_ref.shape[1]

    @pl.when(pl.program_id(0) == 0)
    def _():
        for i in range(2):

            @pl.when(side_ref[1] ^ i == side_ref[2])
            def _(i=i):
                place = pl.multiple_of(side_ref[1] * own, 128)
                own_send_ref[...] = halves[2 * i][:, pl.ds(place, own)]
                own_keep_ref[...] = halves[2 * i + 1][:, pl.ds(place, own)]

            turned[i] = jnp.concatenate([halves[2 * i][...], halves[2 * i + 1][...]], axis=0).T
        lead = jnp.sum(turned[0].astype(F32), axis=0, keepdims=True)
        lead = lead + jnp.sum(turned[1].astype(F32), axis=0, keepdims=True)
        lead_ref[...] = jnp.broadcast_to(lead, lead_ref.shape)

    x = None
    for i in range(2):
        place = pl.multiple_of((side_ref[1] ^ i) * rows, 128)
        part = dot(fields_ref[:, pl.ds(place, rows)], turned[i], 1, 0)
        x = part if x is None else x + part
    x = x.astype(BF).T
    send_ref[...] = x[:half]
    keep_ref[...] = x[half:]


def embed_back(sides, got, fields, own, after):
    rows = got[0].shape[1]
    half = got[0].shape[0] // 32 * 16
    lines, patches = fields.shape
    block = max(b for b in (1152, 576, 384, 128) if lines % b == 0)
    operands = [x for x in got for _ in range(2)]
    specs = [
        pl.BlockSpec((half, rows), lambda i, c, flip=flip: (c[0] ^ flip, 0)) for _ in got for flip in (1, 0)
    ]
    out = pl.BlockSpec((half, block), lambda i, c: (0, i))
    out_shape = [shape(half, lines)] * 2 + [shape(half, own)] * 2 + [shape(8, 2 * half, kind=F32)]
    return call(
        embed_back_kernel,
        "embed_back",
        out_shape,
        [*specs, pl.BlockSpec((block, patches), lambda i, c: (i, 0))],
        [out, out, *[whole(a) for a in out_shape[2:]]],
        grid=(lines // block,),
        scratch=[pltpu.VMEM((2, rows, 2 * half), BF)],
        scalars=1,
        cost=100,
        after=after,
    )(sides, *operands, fields)


def start_back_kernel(frames, keep_ref, core_ref, chan_ref, start_ref, gain_ref, mid_ref, out_ref):
    rows, width = start_ref.shape
    grad = keep_ref[...] + core_ref[...].astype(F32) + chan_ref[...].astype(F32)
    n, r = norm_parts(start_ref[...])
    start = mid_ref[...] + norm_back(grad, n, r, gain_ref[...])
    turned = start.T
    per = width // frames
    turned = [turned[f * per : (f + 1) * per] for f in (*range(0, frames, 2), *range(1, frames, 2))]
    out_ref[:width, :] = jnp.concatenate(turned, axis=0).astype(BF)
    lines = []
    for x in (grad * n, grad):
        x = jnp.sum(x, axis=0, keepdims=True)
        lines += [x[:, j : j + rows] for j in range(0, width, rows)]
    lines.append(jnp.zeros((16 - len(lines), rows), F32))
    out_ref[width:, :] = jnp.concatenate(lines, axis=0).astype(BF)


def start_back(frames, keep, core, far, start, gain, mid_grad, after):
    rows, width = start.shape
    operands = [keep, core, far, start, gain[None], mid_grad]
    out_shape = shape(width + 16, rows)
    return call(
        partial(start_back_kernel, frames),
        "start_back",
        out_shape,
        [pl.BlockSpec((rows, width), lambda i: (0, 0))] * 2 + [whole(a) for a in operands[2:]],
        whole(out_shape),
        grid=(1,),
        cost=100,
        after=after,
    )(*operands)


def pull_kernel(chunk_ref, fields_ref, cot_ref, offset_ref, *rest):
    chunk, step = pl.program_id(0), pl.program_id(1)
    outs, total = rest[:-1], rest[-1]

    @pl.when(step == 0)
    def _():
        total[...] = jnp.zeros_like(total)

    high = 16
    for i in range(0, PIX, high):
        lines = slice(i, i + high)
        sums = [total[e * PIX + i : e * PIX + i + high, :] for e in range(EXP - 1)]
        for c in range(cot_ref.shape[0]):
            g = cot_ref[c, lines, :].astype(F32)
            first = fields_ref[0, c, lines, :].astype(F32)
            shift = offset_ref[0, c, lines, :]
            for e in range(EXP - 1):
                x = fields_ref[e + 1, c, lines, :].astype(F32) - first
                sums[e] = sums[e] + g * (x + (offset_ref[e + 1, c, lines, :] - shift))
        for e in range(EXP - 1):
            total[e * PIX + i : e * PIX + i + high, :] = sums[e]

    for s, out_ref in enumerate(outs):

        @pl.when((step == pl.num_programs(1) - 1) & (chunk == s))
        def _(out_ref=out_ref):
            out_ref[...] = total[...].astype(BF)


def pull(numbers, fields, cot, offset):
    chan = numbers.shape[0]
    channels, pixels, patches = cot.shape
    rows = patches // chan
    block = max(b for b in (6, 3, 2, 1) if channels % b == 0)
    high = (EXP - 1) * PIX
    return call(
        pull_kernel,
        "pull",
        [shape(high, rows)] * chan,
        [
            pl.BlockSpec((EXP, block, PIX, rows), lambda s, i, r: (0, i, 0, r[s])),
            pl.BlockSpec((block, PIX, rows), lambda s, i, r: (i, 0, r[s])),
            pl.BlockSpec((EXP, block, PIX, 1), lambda s, i, r: (0, i, 0, 0)),
        ],
        [pl.BlockSpec((high, rows), lambda s, i, r: (0, 0))] * chan,
        grid=(chan, channels // block),
        scratch=[pltpu.VMEM((high, rows), F32)],
        scalars=1,
    )(numbers, fields, cot, offset)


def blend_kernel(chunk_ref, *refs):
    gate_refs, (fields_ref, cot_ref, offset_ref, mixed_ref, bias_ref, gates_ref) = refs[:2], refs[2:]
    channels, _, patches = cot_ref.shape
    wide, rows = EXP * PIX, gate_refs[0].shape[1]

    @pl.when(pl.program_id(0) == 0)
    def _():
        for i, gate_ref in enumerate(gate_refs):
            place = pl.multiple_of((chunk_ref[0] ^ i) * rows, 128)
            gates_ref[:, pl.ds(place, rows)] = gate_ref[:wide, :]

    high, across = 16, 384
    for i in range(0, PIX, high):
        lines = slice(i, i + high)
        for j in range(0, patches, across):
            cols = slice(j, j + across)
            gates = [gates_ref[e * PIX + i : e * PIX + i + high, cols].astype(F32) for e in range(EXP)]
            for c in range(channels):
                mixed = None
                for e in range(EXP):
                    x = fields_ref[e, c, lines, cols].astype(F32) + offset_ref[e, c, lines, :]
                    term = gates[e] * x
                    mixed = term if mixed is None else mixed + term
                mixed_ref[c, lines, cols] = mixed.astype(BF)
    here = lax.broadcasted_iota(jnp.int32, (PIX, wide), 0)
    there = lax.broadcasted_iota(jnp.int32, (PIX, wide), 1) % PIX
    x = dot(cot_ref[...].reshape(channels * PIX, patches), gates_ref[...], 1, 1)
    for c in range(channels):
        part = jnp.where(here == there, x[c * PIX : (c + 1) * PIX], 0.0)
        bias_ref[0, c : c + 1, :] = jnp.sum(part, axis=0, keepdims=True)


def blend(chunk, gates, fields, cot, offset, after):
    channels, pixels, patches = cot.shape
    block = max(b for b in (6, 3, 2, 1) if channels % b == 0)
    steps = channels // block
    out_shape = [shape(*cot.shape), shape(steps, block, EXP * PIX, kind=F32), shape(EXP * PIX, patches)]
    return call(
        blend_kernel,
        "blend",
        out_shape,
        [
            *[whole(a) for a in gates],
            pl.BlockSpec((EXP, block, PIX, patches), lambda i, c: (0, i, 0, 0)),
            pl.BlockSpec((block, PIX, patches), lambda i, c: (i, 0, 0)),
            pl.BlockSpec((EXP, block, PIX, 1), lambda i, c: (0, i, 0, 0)),
        ],
        [
            pl.BlockSpec((block, PIX, patches), lambda i, c: (i, 0, 0)),
            pl.BlockSpec((1, block, EXP * PIX), lambda i, c: (i, 0, 0)),
            whole(out_shape[2]),
        ],
        grid=(steps,),
        scalars=1,
        after=after,
    )(chunk, *gates, fields, cot, offset)


def fields_back_kernel(frames, chunk_ref, weight_ref, turned_ref, gate_ref, cot_ref, *rest):
    out_ref, start = rest[-2:]
    width = weight_ref.shape[2]
    per = width // frames

    @pl.when(pl.program_id(0) == 0)
    def _():
        x = turned_ref[:width, :].astype(F32)
        order = [(f % 2) * (frames // 2) + f // 2 for f in range(frames)]
        start[...] = jnp.concatenate([x[g * per : (g + 1) * per] for g in order], axis=0).astype(BF)

    grad = dot(weight_ref[0], start[...], 1, 0)
    gate = gate_ref[...].astype(F32)
    for c in range(cot_ref.shape[0]):
        lines = slice(c * PIX, (c + 1) * PIX)
        out_ref[0, lines, :] = (grad[lines, :] + gate * cot_ref[c].astype(F32)).astype(BF)


def fields_back(frames, chunk, weight, turned, gates, cot, grad, after):
    channels, pixels, patches = cot.shape
    rows = turned.shape[1]
    width = weight.shape[2]
    in_specs = [
        pl.BlockSpec((1, channels * PIX, width), lambda e, r: (e, 0, 0)),
        whole(turned),
        pl.BlockSpec((PIX, rows), lambda e, r: (e, r[0])),
        pl.BlockSpec((channels, PIX, rows), lambda e, r: (0, 0, r[0])),
    ]
    operands = [chunk, weight, turned, gates, cot]
    more = {}
    if grad is not None:
        in_specs.append(pl.BlockSpec(memory_space=pl.ANY))
        operands.append(grad)
        more = {"input_output_aliases": {5: 0}}
    return call(
        partial(fields_back_kernel, frames),
        "fields_back",
        shape(EXP, channels * PIX, patches),
        in_specs,
        pl.BlockSpec((1, channels * PIX, rows), lambda e, r: (e, 0, r[0])),
        grid=(EXP,),
        scratch=[pltpu.VMEM((width, rows), BF)],
        scalars=1,
        after=after,
        **more,
    )(*operands)


def norm_parts(v):
    centred = v - jnp.mean(v, axis=-1, keepdims=True)
    spread = jnp.mean(centred * centred, axis=-1, keepdims=True)
    r = lax.rsqrt(spread + epsilon)
    return centred * r, r


def norm_back(grad, n, r, gain):
    t = grad * gain
    return r * (
        t - jnp.mean(t, axis=-1, keepdims=True) - n * jnp.mean(t * n, axis=-1, keepdims=True)
    )


def add_low(a, b):
    return (a.astype(F32) + b.astype(F32)).astype(BF)


def halve(x, axis, mine):
    keep = lax.dynamic_index_in_dim(x, mine, axis, keepdims=False)
    send = lax.dynamic_index_in_dim(x, 1 - mine, axis, keepdims=False)
    return keep, send


def merge_kernel(blocks, side_ref, *refs):
    ins, (send_ref, keep_ref) = refs[:-2], refs[-2:]

    def put(gone, gone_far, kept, kept_far):
        for a, b, out_ref in ((gone, gone_far, send_ref), (kept, kept_far, keep_ref)):
            x = a[...].astype(F32) + b[...].astype(F32)
            out_ref[...] = x.astype(BF).reshape(out_ref.shape)

    if blocks == 0:
        (gone, kept), n = ins[:2], len(ins) // 2 - 1
        for i in range(n):
            far = ins[2 + i], ins[2 + n + i]
            pl.when(pl.program_id(0) == i)(lambda far=far: put(gone, far[0], kept, far[1]))
    elif len(ins) == 4:
        put(*ins)
    else:
        pl.when(pl.program_id(0) < blocks)(lambda: put(*ins[:4]))
        pl.when(pl.program_id(0) == blocks)(lambda: put(*ins[4:]))


def merge(keep, far, side, window, more, cost, after):
    a, _, rows, n = keep.shape
    first, count = window or (0, n)
    if isinstance(far, list):
        return merge_parts(keep, far, side, after)
    block = more[0].shape[3] if more else max(
        b for b in (1024, 768, 640, 384, 256, 128) if count % b == 0 and first % b == 0 and (b < count or b < 512)
    )
    blocks = count // block
    specs = [
        pl.BlockSpec(
            (a, 1, rows, block),
            lambda i, c, flip=flip: (0, c[0] ^ flip, 0, jnp.minimum(i, blocks - 1) + first // block),
        )
        for flip in (1, 1, 0, 0)
    ]
    operands = [keep, far, keep, far]
    if more:
        specs += [
            pl.BlockSpec((a, 1, rows, block), lambda i, c, flip=flip: (0, c[0] ^ flip, 0, 0))
            for flip in (1, 1, 0, 0)
        ]
        operands += [*more, *more]
    steps = blocks + (1 if more else 0)
    out = pl.BlockSpec((a, rows, block), lambda i, c: (0, 0, i))
    return call(
        partial(merge_kernel, blocks),
        "merge",
        [shape(a, rows, steps * block)] * 2,
        specs,
        [out, out],
        grid=(steps,),
        scalars=1,
        cost=cost,
        after=after,
    )(side.astype(jnp.int32)[None], *operands)


def merge_parts(keep, far, side, after):
    a, _, rows, n = keep.shape
    block = n // len(far)

    def spec(flip, step):
        return pl.BlockSpec((a, 1, rows, block), lambda i, c: (0, c[0] ^ flip, 0, i * step))

    out = pl.BlockSpec((a, rows, block), lambda i, c: (0, 0, i))
    return call(
        partial(merge_kernel, 0),
        "merge",
        [shape(a, rows, n)] * 2,
        [spec(1, 1), spec(0, 1), *[spec(1, 0) for _ in far], *[spec(0, 0) for _ in far]],
        [out, out],
        grid=(len(far),),
        scalars=1,
        after=after,
    )(side.astype(jnp.int32)[None], keep, keep, *far, *far)


class Sum:
    def __init__(self, plan, f, z, order, keep, far, window=None, more=None):
        self.plan, self.at, self.order = plan, {"f": f, "z": z}, list(order)
        self.left = sorted(order, key=lambda b: (b[0] != "f", -b[1]))
        self.keep, self.far, self.window, self.more = keep, far, window, more

    def step(self, after, cost=0):
        axis, bit = self.order.pop(0)
        a = 2 ** self.left.index((axis, bit))
        def rows(x):
            return [rows(y) for y in x] if isinstance(x, list) else x.reshape(a, 2, -1, x.shape[-1])

        keep, far, *more = (rows(x) for x in (self.keep, self.far, *(self.more or ())))
        side = (self.at[axis] // bit) % 2
        send, self.keep = merge(keep, far, side, self.window, more, cost, after)
        self.far = (self.plan.swap_frame if axis == "f" else self.plan.swap_chan)(send, bit)
        self.window = self.more = None
        self.left.remove((axis, bit))
        return send

    def finish(self):
        while self.order:
            self.step([])
        n = self.keep.shape[-1]
        return self.keep.reshape(-1, n).astype(F32) + self.far.reshape(-1, n).astype(F32)


def on_device(
    plan,
    fields,
    lead_index,
    embed_weight,
    position_embed,
    lead_table,
    attend_gain,
    attend_shift,
    attend_weight,
    out_weight,
    out_bias,
    mixer_gain,
    mixer_shift,
    up_weight,
    up_bias,
    down_weight,
    down_bias,
    head_weight,
    specialist_cell_offset,
    cotangent,
):
    f, z = lax.axis_index("frames"), lax.axis_index("chan")
    chan, frames = plan.chan, plan.frames
    width = attend_gain.shape[0]
    hidden_width = up_bias.shape[0]
    channels, pixels, patches = cotangent.shape[1:]
    rows = position_embed.shape[0]
    lines = EXP * channels * PIX
    own_fields, cot = fields[0], cotangent[0]
    flat_fields = own_fields.reshape(lines, patches)
    flat_weight = embed_weight.reshape(lines, width)
    offset = specialist_cell_offset[..., None]
    numbers = jnp.stack([z ^ s for s in range(chan)]).astype(jnp.int32)
    mine = (f % 2).astype(jnp.int32)[None]

    onehot = (
        lead_index[:, None] == jnp.arange(lead_table.shape[0], dtype=jnp.int32)[None, :]
    ).astype(BF)
    lead_vector = dot(onehot, lead_table, 1, 0)
    got = []
    for s in reversed(range(chan)):
        block = lax.dynamic_slice(flat_fields, (0, (z ^ s) * rows), (lines, rows))
        part = dot(block, flat_weight, 0, 0)
        if s == 0:
            part = part + position_embed.astype(F32) + lead_vector
        got.append(plan.to_worker(part.astype(BF), s))

    def flag(x):
        return x.astype(jnp.int32)[None]

    core, low = f % 2, z % 2

    pulls = pull(numbers, own_fields, cot, offset)
    vectors = jnp.concatenate([out_bias, mixer_gain, mixer_shift, down_bias, up_bias])[None]

    stream_start, normed = first_norm(got, attend_gain, attend_shift, [pulls[0], vectors])
    normed_chan = plan.swap_chan(normed, 1)
    near, near_turned, queries = project(normed, plan.swap_frame(normed, 1), attend_weight, True, [])
    pulls = [plan.to_worker(a, s) for s, a in enumerate(pulls)]
    (normed_chan,) = relay([normed_chan], [near])
    far, far_turned = project(normed_chan, plan.swap_frame(normed_chan, 1), attend_weight, False, [])
    attended, attended_turned, shares, rinv = attend(queries, near, far)

    (
        gate, _, mid_grad, attended_low, normed_turned, end_turned, down_low, logit_low, branch_low,
        active_turned, hidden_low,
    ) = middle(stream_start, attended, out_weight, vectors, head_weight, pulls, up_weight, down_weight)

    gate = plan.from_workers(beside(flag(core), gate, plan.swap_frame(gate, 1), []))

    query_low, keep_grad, send_grad = attend_back(queries, near, far, attended, attended_low, shares, rinv, [])
    send = project_back(send_grad, attend_weight, gate)
    keep = project_back(keep_grad, attend_weight, [send], query_low)
    send = plan.swap_frame(send, 1)
    far_grad = (keep[rows:] + send[rows:].astype(F32)).astype(BF)
    going = [far_grad]
    far_grad = plan.swap_chan(far_grad, 1)

    n_wide = hidden_width + (-hidden_width % WIDE) + WIDE
    weights = tall_grads(frames, chan, active_turned, down_low, n_wide, going)
    weights = wide_grads(normed_turned, hidden_low, attended_turned, branch_low, end_turned, logit_low, weights)
    step = weights
    weights = lax.psum_scatter(weights, "frames", scatter_dimension=0, tiled=True)

    sent = start_back(frames, keep, send, far_grad, stream_start, attend_gain, mid_grad, [step])
    sent = beside(flag(core), sent, plan.swap_frame(sent, 1), [])
    got = plan.from_workers(sent)

    *attend_send, attend_keep = attend_grads(
        frames, mine, near_turned, far_turned, query_low, keep_grad, send_grad, [sent]
    )
    high = [("f", bit) for bit in bits_of(frames)[1:]]
    lower = [("z", bit) for bit in bits_of(chan)]
    projections = Sum(plan, f, z, high + lower, attend_keep, [plan.swap_frame(a, 1) for a in attend_send])

    mixed, expert_bias, gates = blend(flag(low), gate, own_fields, cot, offset, attend_send)

    step = projections.step([mixed])
    sides = jnp.concatenate([mine, flag(low), flag(z // plan.half)])
    embed_send, embed_keep, own_send, own_keep, lead = embed_back(sides, got, flat_fields, rows, [step])
    embed_far, own_far = plan.swap_frame(embed_send, 1), plan.swap_frame(own_send, 1)
    cut = (lines // rows + 1) // 2 * rows
    embed_sums = [
        Sum(plan, f, z, high, embed_keep, embed_far, (0, cut)),
        Sum(plan, f, z, high[::-1], embed_keep, embed_far, (cut, lines - cut), (own_keep, own_far)),
    ]
    step = projections.step([embed_send], 30)
    step = embed_sums[0].step([step])
    step = embed_sums[1].step([step])
    (weights,) = relay([weights], [step])
    step = weights
    weights = lax.psum_scatter(weights, "chan", scatter_dimension=0, tiled=True)
    wide_weight = embed_weight.reshape(EXP, channels * PIX, width)
    fields_grad = fields_back(frames, flag(low), wide_weight, got[0], gates, cot, None, [step])

    per = width // frames
    lead = lead[0].reshape(2, frames // 2, per)
    lead = jnp.swapaxes(jnp.where(core == 0, lead[::-1], lead), 0, 1).reshape(-1, rows)
    own = (jnp.arange(frames) == f).astype(F32)
    n_lead = lead.shape[0]
    parts = [
        sum(a[EXP * PIX :, i : i + rows].astype(F32) for a in gate for i in (0, rows)),
        sum(a[width : width + 2 * n_lead, i : i + rows].astype(F32) for a in got for i in (0, rows)),
        (own[:, None, None] * lead).reshape(-1, rows),
        jnp.pad(own * lead_index.astype(F32), (0, rows - frames))[None],
        expert_bias.reshape(-1, rows),
    ]
    small = jnp.concatenate(parts, axis=0)
    (small,) = relay([jnp.pad(small, ((0, -small.shape[0] % 16), (0, 0))).astype(BF)], [fields_grad])
    others = iter(bits_of(frames))
    small_far = plan.swap_frame(small, next(others))
    fields_grad = fields_back(frames, flag(1 - low), wide_weight, got[1], gates, cot, fields_grad, [small])
    step = projections.step([fields_grad])
    step = embed_sums[0].step([step]) if embed_sums[0].order else step
    step = embed_sums[1].step([step, weights]) if embed_sums[1].order else step
    step = projections.step([step])
    for i, bit in enumerate(others):
        small = plus(small, small_far, [step])
        small_far = plan.swap_frame(small, bit)
        step = small

    weights = weights.astype(F32)
    small = small.astype(F32) + small_far.astype(F32)
    cuts, first = [], 0
    for a in parts:
        cuts.append(small[first : first + a.shape[0]])
        first += a.shape[0]
    vectors, norms, lead, index, bias = cuts
    here = f * chan + z
    n_each = width // (frames * chan)

    def own_part(x, n=n_each, axis=0):
        return lax.dynamic_slice_in_dim(x, here * n, n, axis)

    vectors_out = jnp.concatenate([vectors[: 4 * n_lead], norms], axis=0).reshape(6, width)
    vectors_out = own_part(vectors_out, axis=1)
    up_bias_out = own_part(vectors[4 * n_lead :].reshape(-1), hidden_width // (frames * chan))
    rows_of_table = index[0, :frames, None] == jnp.arange(lead_table.shape[0], dtype=F32)[None]
    lead = own_part(lead.reshape(frames, width), axis=1)
    table_out = jnp.sum(rows_of_table[:, :, None].astype(F32) * lead[:, None, :], axis=0)
    bias = lax.dynamic_slice_in_dim(bias.reshape(channels, EXP, PIX), f * (PIX // frames), PIX // frames, 2)
    bias_out = jnp.swapaxes(bias, 0, 1)
    first, second = (a.finish() for a in embed_sums)
    n = lines - first.shape[1]
    embed_out = jnp.concatenate([first, second[:, :n]], axis=1).T.reshape(EXP, channels, PIX, per)
    position_out = second[:, n:].T
    attend_out = projections.finish()
    tall = weights[:, :hidden_width].reshape(n_each, -1, width)
    tall = jnp.swapaxes(tall, 0, 1).reshape(-1, width)
    wide = weights[:, hidden_width:]

    return (
        mixed[None],
        fields_grad.reshape(fields.shape),
        embed_out,
        position_out,
        table_out,
        vectors_out[4],
        vectors_out[5],
        attend_out,
        wide[:, hidden_width : hidden_width + width],
        vectors_out[2],
        vectors_out[0],
        vectors_out[1],
        wide[:, :hidden_width],
        up_bias_out,
        tall,
        vectors_out[3],
        wide[:, hidden_width + width : hidden_width + width + EXP * PIX],
        bias_out,
    )


def solution(mesh):
    plan = Plan(mesh.shape["frames"], mesh.shape["chan"])
    both = ("frames", "chan")
    in_specs = (
        P("frames", None, "chan", None, None),
        P("frames"),
        P(None, "chan", None, None),
        P("chan", None),
        *[P()] * 13,
        P(None, "chan", None),
        P("frames", "chan", None, None),
    )
    out_specs = (
        P("frames", "chan", None, None),
        P("frames", None, "chan", None, None),
        P(None, "chan", None, "frames"),
        P("chan", "frames"),
        P(None, both),
        P(both),
        P(both),
        P(both, None),
        P(both, None),
        P(both),
        P(both),
        P(both),
        P(both, None),
        P(both),
        P(both, None),
        P(both),
        P(both, None),
        P(None, "chan", "frames"),
    )
    return jax.shard_map(
        partial(on_device, plan), mesh=mesh, in_specs=in_specs, out_specs=out_specs, check_vma=False
    )
```

```python
from functools import partial

import jax
import jax.numpy as jnp
from jax import lax
from jax.experimental import pallas as pl
from jax.experimental.pallas import tpu as pltpu
from jax.sharding import PartitionSpec as P

HEADS = 12
HEAD_DIM = 64
EXP = 3
PIX = 64
LOG2E = 1.4426950408889634

epsilon = 1e-05
BF = jnp.bfloat16
F32 = jnp.float32


def dot(left, right, left_dim, right_dim):
    return lax.dot_general(
        left, right, (((left_dim,), (right_dim,)), ((), ())), preferred_element_type=F32
    )


class Plan:
    def __init__(self, frames, chan):
        self.frames, self.chan, self.half = frames, chan, chan // 2

    def pairs(self, target):
        return [
            (f * self.chan + z, (lambda t: t[0] * self.chan + t[1])(target(f, z)))
            for f in range(self.frames)
            for z in range(self.chan)
        ]

    def swap_frame(self, x, bit):
        return lax.ppermute(x, ("frames", "chan"), self.pairs(lambda f, z: (f ^ bit, z)))

    def swap_chan(self, x, bit):
        return lax.ppermute(x, ("frames", "chan"), self.pairs(lambda f, z: (f, z ^ bit)))

    def worker(self, f, r):
        return (f & ~1) + r % 2, (f & 1) * self.half + r // 2

    def to_worker(self, x, s):
        return lax.ppermute(
            x, ("frames", "chan"), self.pairs(lambda f, z: self.worker(f, z ^ s))
        )

    def from_workers(self, pair):
        return [
            lax.ppermute(x, ("frames", "chan"), self.sources(lambda f, z: self.holder(f, z, i)))
            for i, x in enumerate((pair, pair))
        ]

    def holder(self, f, z, i):
        return (f & ~1) + z // self.half, (f & 1) * self.half + (z + i) % self.half

    def sources(self, source):
        return [(a, b) for b, a in self.pairs(source)]


def bits_of(n):
    return [1 << i for i in range(n.bit_length() - 1)]


VMEM = 52 << 20


def call(kernel, name, out_shape, in_specs, out_specs, grid=(), scratch=(), scalars=0, cost=0, after=(), **more):
    n_in = scalars + len(in_specs)

    def body(*refs):
        kernel(*refs[:n_in], *refs[n_in + len(after) :])

    run = pl.pallas_call(
        body,
        grid_spec=pltpu.PrefetchScalarGridSpec(
            num_scalar_prefetch=scalars,
            grid=grid,
            in_specs=[*in_specs, *[pl.BlockSpec(memory_space=pl.ANY) for _ in after]],
            out_specs=out_specs,
            scratch_shapes=scratch,
        ),
        out_shape=out_shape,
        compiler_params=pltpu.CompilerParams(vmem_limit_bytes=VMEM),
        cost_estimate=pl.CostEstimate(flops=1 + cost * 10**9, bytes_accessed=1, transcendentals=0),
        name=name,
        **more,
    )
    return lambda *operands: run(*operands, *after)


def shape(*dims, kind=BF):
    return jax.ShapeDtypeStruct(dims, kind)


def whole(x):
    return pl.BlockSpec(x.shape, lambda *_: (0,) * len(x.shape))


def first_norm_kernel(a_ref, b_ref, c_ref, d_ref, gain_ref, shift_ref, start_ref, normed_ref):
    start = sum(x[...].astype(F32) for x in (a_ref, b_ref, c_ref, d_ref))
    start_ref[...] = start
    n, _ = norm_parts(start)
    normed_ref[...] = (n * gain_ref[...] + shift_ref[...]).astype(BF)


def first_norm(parts, gain, shift, after):
    rows, width = parts[0].shape
    operands = [*parts, gain[None], shift[None]]
    out_shape = [shape(rows, width, kind=F32), shape(rows, width)]
    return call(
        first_norm_kernel,
        "first_norm",
        out_shape,
        [whole(a) for a in operands],
        [whole(a) for a in out_shape],
        after=after,
    )(*operands)


def project_kernel(first, near_ref, far_ref, weight_ref, kv_ref, turned_ref, *rest):
    rows = near_ref.shape[0]
    pairs, _, lanes = kv_ref.shape
    step = pl.program_id(0)

    def put():
        for i, x_ref in enumerate((near_ref, far_ref)):
            x = dot(x_ref[...], weight_ref[...], 1, 0).astype(BF)
            for p in range(pairs):
                kv_ref[p, i * rows : (i + 1) * rows, :] = x[:, p * lanes : (p + 1) * lanes]

    @pl.when(step == 0)
    def _():
        for i, x_ref in enumerate((near_ref, far_ref)):
            turned_ref[:, i * rows : (i + 1) * rows] = x_ref[...].T

    if first:

        @pl.when(step == 0)
        def _():
            rest[0][...] = dot(near_ref[...], weight_ref[...], 1, 0).astype(BF)

        pl.when(step > 0)(put)
    else:
        put()


def project(near, far, weight, first, after):
    rows, width = near.shape
    pair = 2 * HEAD_DIM
    pairs = width // pair
    skip = 0 if first else 1
    out_shape = [shape(2 * pairs, 2 * rows, pair), shape(width, 2 * rows)]
    out_specs = [
        pl.BlockSpec((pairs, 2 * rows, pair), lambda i: (jnp.maximum(i + skip - 1, 0), 0, 0)),
        whole(out_shape[1]),
    ]
    if first:
        out_shape.append(shape(rows, width))
        out_specs.append(whole(out_shape[2]))
    return call(
        partial(project_kernel, first),
        "project",
        out_shape,
        [whole(near), whole(far), pl.BlockSpec((width, width), lambda i: (0, i + skip))],
        out_specs,
        grid=(3 - skip,),
        after=after,
    )(near, far, weight)


def attend_kernel(
    q_ref, near_ref, far_ref, near_value_ref, far_value_ref, o_ref, turned_ref, e_ref, rinv_ref
):
    scale = HEAD_DIM ** (-0.5) * LOG2E
    lanes = q_ref.shape[1]
    for h in range(lanes // HEAD_DIM):
        cols = slice(h * HEAD_DIM, (h + 1) * HEAD_DIM)
        q = q_ref[:, cols]
        s_near = dot(q, near_ref[0, :, cols], 1, 1)
        s_far = dot(q, far_ref[0, :, cols], 1, 1)
        m = jnp.maximum(
            jnp.max(s_near, axis=1, keepdims=True), jnp.max(s_far, axis=1, keepdims=True)
        )
        e_near = jnp.exp2((s_near - m) * scale)
        e_far = jnp.exp2((s_far - m) * scale)
        total = jnp.sum(e_near, axis=1, keepdims=True) + jnp.sum(e_far, axis=1, keepdims=True)
        e_near, e_far = e_near.astype(BF), e_far.astype(BF)
        keys = e_near.shape[1]
        e_ref[h, :, :keys] = e_near
        e_ref[h, :, keys:] = e_far
        o = dot(e_near, near_value_ref[0, :, cols], 1, 0) + dot(e_far, far_value_ref[0, :, cols], 1, 0)
        rinv = jnp.broadcast_to(1.0 / total, o.shape)
        rinv_ref[:, cols] = rinv
        o_ref[:, cols] = (o * rinv).astype(BF)
    turned_ref[...] = o_ref[...].T


def attend(q, near, far):
    rows, width = q.shape
    keys = near.shape[1]
    lanes = 2 * HEAD_DIM
    steps = width // lanes
    row_spec = pl.BlockSpec((rows, lanes), lambda i: (0, i))
    key_spec = pl.BlockSpec((1, keys, lanes), lambda i: (i, 0, 0))
    value_spec = pl.BlockSpec((1, keys, lanes), lambda i: (i + steps, 0, 0))
    e_spec = pl.BlockSpec((2, rows, 2 * keys), lambda i: (i, 0, 0))
    return call(
        attend_kernel,
        "attend",
        [
            shape(rows, width),
            shape(width, rows),
            shape(HEADS, rows, 2 * keys),
            shape(rows, width, kind=F32),
        ],
        [row_spec, key_spec, key_spec, value_spec, value_spec],
        [row_spec, pl.BlockSpec((lanes, rows), lambda i: (i, 0)), e_spec, row_spec],
        grid=(steps,),
    )(q, near, far, near, far)


def attend_back_kernel(
    q_ref, near_ref, far_ref, near_value_ref, far_value_ref, o_ref, do_ref, e_ref, rinv_ref,
    dq_ref, keep_ref, send_ref,
):
    scale = HEAD_DIM ** (-0.5)
    rows, lanes = q_ref.shape
    for h in range(lanes // HEAD_DIM):
        cols = slice(h * HEAD_DIM, (h + 1) * HEAD_DIM)
        q = q_ref[:, cols]
        do = do_ref[:, cols].astype(F32) * rinv_ref[:, cols]
        inner = jnp.sum(do * o_ref[:, cols].astype(F32), axis=1, keepdims=True)
        do = do.astype(BF)
        dq = None
        for i, (k_ref, v_ref) in enumerate(((near_ref, near_value_ref), (far_ref, far_value_ref))):
            keys = k_ref.shape[1]
            e = e_ref[h, :, i * keys : (i + 1) * keys]
            dp = dot(do, v_ref[0, :, cols], 1, 1)
            ds = (e.astype(F32) * (dp - inner)).astype(BF)
            part = dot(ds, k_ref[0, :, cols], 1, 0)
            dq = part if dq is None else dq + part
            dk = (dot(ds, q, 0, 0) * scale).astype(BF)
            dv = dot(e, do, 0, 0).astype(BF)
            lines = slice(i * rows, (i + 1) * rows)
            for k, x in enumerate((dk, dv)):
                keep_ref[k, 0, lines, cols] = x[:rows]
                send_ref[k, 0, lines, cols] = x[rows:]
        dq_ref[:, cols] = (dq * scale).astype(BF)


def attend_back(q, near, far, o, do, e, rinv, after):
    rows, width = q.shape
    keys = near.shape[1]
    lanes = 2 * HEAD_DIM
    steps = width // lanes
    row_spec = pl.BlockSpec((rows, lanes), lambda i: (0, i))
    key_spec = pl.BlockSpec((1, keys, lanes), lambda i: (i, 0, 0))
    value_spec = pl.BlockSpec((1, keys, lanes), lambda i: (i + steps, 0, 0))
    e_spec = pl.BlockSpec((2, rows, 2 * keys), lambda i: (i, 0, 0))
    return call(
        attend_back_kernel,
        "attend_back",
        [shape(rows, width), *[shape(2, steps, keys, lanes)] * 2],
        [row_spec, key_spec, key_spec, value_spec, value_spec, row_spec, row_spec, e_spec, row_spec],
        [row_spec, *[pl.BlockSpec((2, 1, keys, lanes), lambda i: (0, i, 0, 0))] * 2],
        grid=(steps,),
        after=after,
    )(q, near, far, near, far, o, do, e, rinv)


def all_pairs(ref, k):
    return jnp.concatenate([ref[k, p] for p in range(ref.shape[1])], axis=1)


def project_back_kernel(grad_ref, weight_ref, *rest):
    step, out_ref = pl.program_id(0), rest[-1]

    @pl.when(step < 2)
    def _():
        x = dot(all_pairs(grad_ref, 0), weight_ref[...], 1, 1)

        @pl.when(step == 0)
        def _():
            rest[-2][...] = x

        @pl.when(step == 1)
        def _():
            out_ref[...] = (rest[-2][...] + x).astype(out_ref.dtype)

    if len(rest) > 2:

        @pl.when(step == 2)
        def _():
            rows = rest[0].shape[0]
            out_ref[:rows, :] += dot(rest[0][...], weight_ref[...], 1, 1)


def project_back(grads, weight, after, *queries):
    _, pairs, rows, lanes = grads.shape
    width = weight.shape[0]
    out_shape = shape(rows, width, kind=F32 if queries else BF)

    def kernel(*refs):
        *ins, out_ref, total = refs
        project_back_kernel(*ins, total, out_ref)

    return call(
        kernel,
        "project_back",
        out_shape,
        [
            pl.BlockSpec((1, pairs, rows, lanes), lambda i: (jnp.minimum(i, 1), 0, 0, 0)),
            pl.BlockSpec((width, width), lambda i: (0, (i + 1) % 3)),
            *[whole(a) for a in queries],
        ],
        whole(out_shape),
        grid=(3 if queries else 2,),
        scratch=[pltpu.VMEM((rows, width), F32)],
        after=after,
    )(grads, weight, *queries)


def relay_kernel(*refs):
    n = len(refs) // 2
    for a, b in zip(refs[:n], refs[n:]):
        b[...] = a[...]


def relay(arrays, after):
    specs = [whole(x) for x in arrays]
    return call(relay_kernel, "relay", [shape(*x.shape) for x in arrays], specs, specs, after=after)(*arrays)


def beside_kernel(core_ref, x_ref, other_ref, out_ref):
    n = x_ref.shape[1]
    for core, (a_ref, b_ref) in enumerate(((x_ref, other_ref), (other_ref, x_ref))):

        @pl.when(core_ref[0] == core)
        def _():
            out_ref[:, :n] = a_ref[...]
            out_ref[:, n:] = b_ref[...]


def beside(core, x, other, after):
    out_shape = shape(x.shape[0], 2 * x.shape[1])
    return call(
        beside_kernel, "beside", out_shape, [whole(x), whole(other)], whole(out_shape), scalars=1, after=after
    )(core, x, other)


def plus_kernel(a_ref, b_ref, out_ref):
    out_ref[...] = (a_ref[...].astype(F32) + b_ref[...].astype(F32)).astype(BF)


def plus(a, b, after):
    return call(plus_kernel, "plus", shape(*a.shape), [whole(a), whole(b)], whole(a), after=after)(a, b)


def middle_kernel(
    start_ref, attended_ref, out_ref, vector_ref, head_ref, pull0_ref, pull1_ref, pull2_ref, pull3_ref, up_any, down_any,
    gate_ref, sum_ref, mid_grad_ref, attended_low_ref, normed_turned_ref, end_turned_ref,
    down_low_ref, logit_low_ref, branch_low_ref, active_any, hidden_any,
    up, down, slope, active_turned, hidden_low, in_sem, out_sem,
):
    rows, width = start_ref.shape
    hidden_width = up.shape[1]
    steps = in_sem.shape[1]
    tile = hidden_width // steps
    tiles = [slice(i * tile, (i + 1) * tile) for i in range(steps)]
    ups = [pltpu.make_async_copy(up_any.at[:, t], up.at[:, t], in_sem.at[0, i]) for i, t in enumerate(tiles)]
    downs = [pltpu.make_async_copy(down_any.at[t], down.at[t], in_sem.at[1, i]) for i, t in enumerate(tiles)]
    outs = [
        pltpu.make_async_copy(active_turned.at[t], active_any.at[t], out_sem.at[0, i])
        for i, t in enumerate(tiles)
    ] + [
        pltpu.make_async_copy(hidden_low.at[:, t], hidden_any.at[:, t], out_sem.at[1, i])
        for i, t in enumerate(tiles)
    ]
    for a, b in zip(ups, downs):
        a.start()
        b.start()
    out_bias, gain, shift, down_bias, up_bias = (
        vector_ref[:, width * i : width * (i + 1) if i < 4 else width * 4 + hidden_width] for i in range(5)
    )
    mid = start_ref[...] + dot(attended_ref[...], out_ref[...], 1, 0) + out_bias
    n, r = norm_parts(mid)
    normed = (n * gain + shift).astype(BF)
    normed_turned_ref[...] = normed.T
    end = mid + down_bias
    k, cube = 0.7978845608028654, 0.044715
    for i, t in enumerate(tiles):
        ups[i].wait()
        h = dot(normed, up[:, t], 1, 0) + up_bias[:, t]
        square = h * h
        th = jnp.tanh(h * (k + (k * cube) * square))
        half = 0.5 + 0.5 * th
        active = (h * half).astype(BF)
        slope[:, t] = half + h * (half * (1.0 - th)) * (k + (3 * k * cube) * square)
        active_turned[t, :] = active.T
        outs[i].start()
        downs[i].wait()
        end = end + dot(active, down[t, :], 1, 0)
    end_low = end.astype(BF)
    end_turned_ref[...] = end_low.T

    logits = dot(end_low, head_ref[...], 1, 0).T
    a, b, c = (logits[e * PIX : (e + 1) * PIX] for e in range(EXP))
    m = jnp.maximum(jnp.maximum(a, b), c)
    a, b, c = jnp.exp(a - m), jnp.exp(b - m), jnp.exp(c - m)
    share = 1.0 / (a + b + c)
    a, b, c = a * share, b * share, c * share
    pull = sum(x[...].astype(F32) for x in (pull0_ref, pull1_ref, pull2_ref, pull3_ref))
    second, third = pull[:PIX], pull[PIX:]
    inner = b * second + c * third
    logit_grad = jnp.concatenate([-a * inner, b * (second - inner), c * (third - inner)], axis=0)
    gate_ref[: EXP * PIX, :] = jnp.concatenate([a, b, c], axis=0).astype(BF)
    logit_low_ref[...] = logit_grad.astype(BF)

    end_grad = dot(logit_grad.T.astype(BF), head_ref[...], 1, 1)
    down_low = end_grad.astype(BF)
    down_low_ref[...] = down_low
    second_grad = jnp.zeros((rows, width), F32)
    per = width // rows
    for i, t in enumerate(tiles):
        grad = dot(down_low, down[t, :], 1, 1) * slope[:, t]
        total = jnp.sum(grad, axis=0, keepdims=True)
        for j in range(tile // rows):
            line = 4 * per + (t.start // rows) + j
            sum_ref[line : line + 1, :] = total[:, j * rows : (j + 1) * rows]
        low = grad.astype(BF)
        hidden_low[:, t] = low
        outs[steps + i].start()
        second_grad = second_grad + dot(low, up[:, t], 1, 1)
    mid_grad = end_grad + norm_back(second_grad, n, r, gain)
    mid_grad_ref[...] = mid_grad
    branch = mid_grad.astype(BF)
    branch_low_ref[...] = branch
    attended_low_ref[...] = dot(branch, out_ref[...], 1, 1).astype(BF)
    for i, x in enumerate((second_grad * n, second_grad, mid_grad, end_grad)):
        x = jnp.sum(x, axis=0, keepdims=True)
        for j in range(per):
            sum_ref[i * per + j : i * per + j + 1, :] = x[:, j * rows : (j + 1) * rows]
    gate_ref[EXP * PIX :, :] = sum_ref[...].astype(BF)
    for a in outs:
        a.wait()


def middle(start, attended, out_w, vectors, head_w, pulls, up_w, down_w):
    rows, width = start.shape
    hidden_width = up_w.shape[1]
    steps = 4
    lines = (4 * width + hidden_width) // rows
    operands = [start, attended, out_w, vectors, head_w, *pulls]
    out_shape = [
        shape(EXP * PIX + lines, rows),
        shape(lines, rows, kind=F32),
        shape(rows, width, kind=F32),
        shape(rows, width),
        shape(width, rows),
        shape(width, rows),
        shape(rows, width),
        shape(EXP * PIX, rows),
        shape(rows, width),
        shape(hidden_width, rows),
        shape(rows, hidden_width),
    ]
    any_spec = pl.BlockSpec(memory_space=pl.ANY)
    return call(
        middle_kernel,
        "middle",
        out_shape,
        [*[whole(a) for a in operands], any_spec, any_spec],
        [*[whole(a) for a in out_shape[:-2]], any_spec, any_spec],
        scratch=[
            pltpu.VMEM((width, hidden_width), BF),
            pltpu.VMEM((hidden_width, width), BF),
            pltpu.VMEM((rows, hidden_width), F32),
            pltpu.VMEM((hidden_width, rows), BF),
            pltpu.VMEM((rows, hidden_width), BF),
            pltpu.SemaphoreType.DMA((2, steps)),
            pltpu.SemaphoreType.DMA((2, steps)),
        ],
    )(*operands, up_w, down_w)


def half_rows(x, blocks, mine, flip):
    per = x.shape[0] // blocks
    x = x.reshape(blocks // 2, 2, per, x.shape[1])
    block = (blocks // 2, 1, per, x.shape[3])
    if per % 16 == 0:
        return x, pl.BlockSpec(block, lambda *a: (0, a[-1][0] ^ flip, 0, 0))
    x = lax.dynamic_index_in_dim(x, mine[0] ^ flip, 1, keepdims=False).reshape(1, 1, -1, x.shape[3])
    return x, whole(x)


def rows_of(ref):
    return ref[...].reshape(-1, ref.shape[3])


def both_halves(send_ref, keep_ref):
    return jnp.concatenate([rows_of(send_ref), rows_of(keep_ref)], axis=0)


def tall_grads_kernel(frames, chan, active_ref, down_ref, out_ref):
    lines, width = active_ref.shape[0], down_ref.shape[1]
    x = dot(active_ref[...], down_ref[...], 1, 0)
    across = out_ref.shape[1] // width
    per = lines // (chan * across * frames)
    parts = [
        jnp.concatenate([x[i + k * per : i + (k + 1) * per] for k in range(across)], axis=1)
        for i in range(0, lines, per * across)
    ]
    out_ref[...] = jnp.concatenate(parts, axis=0).astype(BF)


def tall_grads(frames, chan, active, down, wide, after):
    hidden_width, rows = active.shape
    width = down.shape[1]
    at_once = max(1, frames // 4)
    across = hidden_width // width
    return call(
        partial(tall_grads_kernel, at_once, chan),
        "tall_grads",
        shape(width, hidden_width + wide),
        [pl.BlockSpec((at_once * hidden_width // frames, rows), lambda i: (i, 0)), whole(down)],
        pl.BlockSpec((at_once * width // frames, across * width), lambda i: (i, 0)),
        grid=(frames // at_once,),
        after=after,
    )(active, down)


def wide_grads_kernel(normed_ref, hidden_ref, attended_ref, branch_ref, end_ref, logit_ref, tall_ref, out_ref):
    step, last = pl.program_id(0), pl.num_programs(0) - 1

    @pl.when(step < last)
    def _():
        out_ref[...] = dot(normed_ref[...], hidden_ref[...], 1, 0).astype(BF)

    @pl.when(step == last)
    def _():
        x = dot(attended_ref[...], branch_ref[...], 1, 0)
        y = dot(end_ref[...], logit_ref[...], 1, 1)
        spare = out_ref.shape[1] - x.shape[1] - y.shape[1]
        out_ref[...] = jnp.concatenate([x, y, jnp.zeros((x.shape[0], spare), F32)], axis=1).astype(BF)


WIDE = 1024


def wide_grads(normed, hidden, attended, branch, end, logit, tall):
    width, rows = normed.shape
    hidden_width = hidden.shape[1]
    steps = hidden_width // WIDE + 1
    operands = [normed, hidden, attended, branch, end, logit, tall]
    specs = [whole(x) for x in operands]
    specs[1] = pl.BlockSpec((rows, WIDE), lambda i: (0, jnp.minimum(i, steps - 2)))
    specs[6] = pl.BlockSpec(memory_space=pl.ANY)
    return call(
        wide_grads_kernel,
        "wide_grads",
        shape(*tall.shape),
        specs,
        pl.BlockSpec((width, WIDE), lambda i: (0, i + hidden_width // WIDE)),
        grid=(steps,),
        input_output_aliases={6: 0},
    )(*operands)


def attend_grads_kernel(
    side_ref, near_ref, near2_ref, far_ref, far2_ref, query_ref, keep_grad_ref, send_grad_ref, *rest
):
    sends, keep_ref = rest[:-1], rest[-1]
    rows, width = query_ref.shape
    half = keep_ref.shape[0]
    step = pl.program_id(0)
    near, far = both_halves(near_ref, near2_ref), both_halves(far_ref, far2_ref)

    def put(i, x):
        @pl.when(step == i)
        def _():
            sends[i][...] = x[:half].astype(BF)

        keep_ref[...] = x[half:].astype(BF)

    @pl.when(step == 0)
    def _():
        put(0, dot(near[:, :rows], query_ref[...], 1, 0))

    @pl.when(step > 0)
    def _():
        a, b = all_pairs(keep_grad_ref, 0), all_pairs(send_grad_ref, 0)
        x = dot(near[:, :rows], a[:rows], 1, 0) + dot(near[:, rows:], b[:rows], 1, 0)
        x = x + dot(far[:, :rows], a[rows:], 1, 0) + dot(far[:, rows:], b[rows:], 1, 0)
        put(1, x)
        put(2, x)


def attend_grads(frames, mine, near, far, query, keep, send, after):
    rows, width = query.shape
    operands, specs = [], []
    for x in (near, far):
        for part in (half_rows(x, frames, mine, 1), half_rows(x, frames, mine, 0)):
            operands.append(part[0])
            specs.append(part[1])
    grad = pl.BlockSpec((1, *keep.shape[1:]), lambda i, c: (jnp.maximum(i - 1, 0), 0, 0, 0))
    out = pl.BlockSpec((width // 2, width), lambda i, c: (0, i))
    return call(
        attend_grads_kernel,
        "attend_grads",
        [shape(width // 2, width)] * 3 + [shape(width // 2, 3 * width)],
        [*specs, whole(query), grad, grad],
        [pl.BlockSpec((width // 2, width), lambda i, c: (0, 0))] * 3 + [out],
        grid=(3,),
        scalars=1,
        after=after,
    )(mine, *operands, query, keep, send)


def embed_back_kernel(side_ref, *refs):
    halves, (fields_ref, send_ref, keep_ref, own_send_ref, own_keep_ref, lead_ref, turned) = refs[:4], refs[4:]
    half, rows = halves[0].shape
    own = own_send_ref.shape[1]

    @pl.when(pl.program_id(0) == 0)
    def _():
        for i in range(2):

            @pl.when(side_ref[1] ^ i == side_ref[2])
            def _(i=i):
                place = pl.multiple_of(side_ref[1] * own, 128)
                own_send_ref[...] = halves[2 * i][:, pl.ds(place, own)]
                own_keep_ref[...] = halves[2 * i + 1][:, pl.ds(place, own)]

            turned[i] = jnp.concatenate([halves[2 * i][...], halves[2 * i + 1][...]], axis=0).T
        lead = jnp.sum(turned[0].astype(F32), axis=0, keepdims=True)
        lead = lead + jnp.sum(turned[1].astype(F32), axis=0, keepdims=True)
        lead_ref[...] = jnp.broadcast_to(lead, lead_ref.shape)

    x = None
    for i in range(2):
        place = pl.multiple_of((side_ref[1] ^ i) * rows, 128)
        part = dot(fields_ref[:, pl.ds(place, rows)], turned[i], 1, 0)
        x = part if x is None else x + part
    x = x.astype(BF).T
    send_ref[...] = x[:half]
    keep_ref[...] = x[half:]


def embed_back(sides, got, fields, own, after):
    rows = got[0].shape[1]
    half = got[0].shape[0] // 32 * 16
    lines, patches = fields.shape
    block = max(b for b in (1152, 576, 384, 128) if lines % b == 0)
    operands = [x for x in got for _ in range(2)]
    specs = [
        pl.BlockSpec((half, rows), lambda i, c, flip=flip: (c[0] ^ flip, 0)) for _ in got for flip in (1, 0)
    ]
    out = pl.BlockSpec((half, block), lambda i, c: (0, i))
    out_shape = [shape(half, lines)] * 2 + [shape(half, own)] * 2 + [shape(8, 2 * half, kind=F32)]
    return call(
        embed_back_kernel,
        "embed_back",
        out_shape,
        [*specs, pl.BlockSpec((block, patches), lambda i, c: (i, 0))],
        [out, out, *[whole(a) for a in out_shape[2:]]],
        grid=(lines // block,),
        scratch=[pltpu.VMEM((2, rows, 2 * half), BF)],
        scalars=1,
        cost=100,
        after=after,
    )(sides, *operands, fields)


def start_back_kernel(frames, keep_ref, core_ref, chan_ref, start_ref, gain_ref, mid_ref, out_ref):
    rows, width = start_ref.shape
    grad = keep_ref[...] + core_ref[...].astype(F32) + chan_ref[...].astype(F32)
    n, r = norm_parts(start_ref[...])
    start = mid_ref[...] + norm_back(grad, n, r, gain_ref[...])
    turned = start.T
    per = width // frames
    turned = [turned[f * per : (f + 1) * per] for f in (*range(0, frames, 2), *range(1, frames, 2))]
    out_ref[:width, :] = jnp.concatenate(turned, axis=0).astype(BF)
    lines = []
    for x in (grad * n, grad):
        x = jnp.sum(x, axis=0, keepdims=True)
        lines += [x[:, j : j + rows] for j in range(0, width, rows)]
    lines.append(jnp.zeros((16 - len(lines), rows), F32))
    out_ref[width:, :] = jnp.concatenate(lines, axis=0).astype(BF)


def start_back(frames, keep, core, far, start, gain, mid_grad, after):
    rows, width = start.shape
    operands = [keep, core, far, start, gain[None], mid_grad]
    out_shape = shape(width + 16, rows)
    return call(
        partial(start_back_kernel, frames),
        "start_back",
        out_shape,
        [pl.BlockSpec((rows, width), lambda i: (0, 0))] * 2 + [whole(a) for a in operands[2:]],
        whole(out_shape),
        grid=(1,),
        cost=100,
        after=after,
    )(*operands)


def pull_kernel(chunk_ref, fields_ref, cot_ref, offset_ref, *rest):
    chunk, step = pl.program_id(0), pl.program_id(1)
    outs, total = rest[:-1], rest[-1]

    @pl.when(step == 0)
    def _():
        total[...] = jnp.zeros_like(total)

    high = 16
    for i in range(0, PIX, high):
        lines = slice(i, i + high)
        sums = [total[e * PIX + i : e * PIX + i + high, :] for e in range(EXP - 1)]
        for c in range(cot_ref.shape[0]):
            g = cot_ref[c, lines, :].astype(F32)
            first = fields_ref[0, c, lines, :].astype(F32)
            shift = offset_ref[0, c, lines, :]
            for e in range(EXP - 1):
                x = fields_ref[e + 1, c, lines, :].astype(F32) - first
                sums[e] = sums[e] + g * (x + (offset_ref[e + 1, c, lines, :] - shift))
        for e in range(EXP - 1):
            total[e * PIX + i : e * PIX + i + high, :] = sums[e]

    for s, out_ref in enumerate(outs):

        @pl.when((step == pl.num_programs(1) - 1) & (chunk == s))
        def _(out_ref=out_ref):
            out_ref[...] = total[...].astype(BF)


def pull(numbers, fields, cot, offset):
    chan = numbers.shape[0]
    channels, pixels, patches = cot.shape
    rows = patches // chan
    block = max(b for b in (6, 3, 2, 1) if channels % b == 0)
    high = (EXP - 1) * PIX
    return call(
        pull_kernel,
        "pull",
        [shape(high, rows)] * chan,
        [
            pl.BlockSpec((EXP, block, PIX, rows), lambda s, i, r: (0, i, 0, r[s])),
            pl.BlockSpec((block, PIX, rows), lambda s, i, r: (i, 0, r[s])),
            pl.BlockSpec((EXP, block, PIX, 1), lambda s, i, r: (0, i, 0, 0)),
        ],
        [pl.BlockSpec((high, rows), lambda s, i, r: (0, 0))] * chan,
        grid=(chan, channels // block),
        scratch=[pltpu.VMEM((high, rows), F32)],
        scalars=1,
    )(numbers, fields, cot, offset)


def blend_kernel(chunk_ref, *refs):
    gate_refs, (fields_ref, cot_ref, offset_ref, mixed_ref, bias_ref, gates_ref) = refs[:2], refs[2:]
    channels, _, patches = cot_ref.shape
    wide, rows = EXP * PIX, gate_refs[0].shape[1]

    @pl.when(pl.program_id(0) == 0)
    def _():
        for i, gate_ref in enumerate(gate_refs):
            place = pl.multiple_of((chunk_ref[0] ^ i) * rows, 128)
            gates_ref[:, pl.ds(place, rows)] = gate_ref[:wide, :]

    high, across = 16, 384
    for i in range(0, PIX, high):
        lines = slice(i, i + high)
        for j in range(0, patches, across):
            cols = slice(j, j + across)
            gates = [gates_ref[e * PIX + i : e * PIX + i + high, cols].astype(F32) for e in range(EXP)]
            for c in range(channels):
                mixed = None
                for e in range(EXP):
                    x = fields_ref[e, c, lines, cols].astype(F32) + offset_ref[e, c, lines, :]
                    term = gates[e] * x
                    mixed = term if mixed is None else mixed + term
                mixed_ref[c, lines, cols] = mixed.astype(BF)
    here = lax.broadcasted_iota(jnp.int32, (PIX, wide), 0)
    there = lax.broadcasted_iota(jnp.int32, (PIX, wide), 1) % PIX
    x = dot(cot_ref[...].reshape(channels * PIX, patches), gates_ref[...], 1, 1)
    for c in range(channels):
        part = jnp.where(here == there, x[c * PIX : (c + 1) * PIX], 0.0)
        bias_ref[0, c : c + 1, :] = jnp.sum(part, axis=0, keepdims=True)


def blend(chunk, gates, fields, cot, offset, after):
    channels, pixels, patches = cot.shape
    block = max(b for b in (6, 3, 2, 1) if channels % b == 0)
    steps = channels // block
    out_shape = [shape(*cot.shape), shape(steps, block, EXP * PIX, kind=F32), shape(EXP * PIX, patches)]
    return call(
        blend_kernel,
        "blend",
        out_shape,
        [
            *[whole(a) for a in gates],
            pl.BlockSpec((EXP, block, PIX, patches), lambda i, c: (0, i, 0, 0)),
            pl.BlockSpec((block, PIX, patches), lambda i, c: (i, 0, 0)),
            pl.BlockSpec((EXP, block, PIX, 1), lambda i, c: (0, i, 0, 0)),
        ],
        [
            pl.BlockSpec((block, PIX, patches), lambda i, c: (i, 0, 0)),
            pl.BlockSpec((1, block, EXP * PIX), lambda i, c: (i, 0, 0)),
            whole(out_shape[2]),
        ],
        grid=(steps,),
        scalars=1,
        after=after,
    )(chunk, *gates, fields, cot, offset)


def fields_back_kernel(frames, chunk_ref, weight_ref, a_ref, b_ref, gate_ref, cot_ref, out_ref, start):
    width = weight_ref.shape[2]
    per = width // frames
    order = [(f % 2) * (frames // 2) + f // 2 for f in range(frames)]
    for i, turned_ref in enumerate((a_ref, b_ref)):

        @pl.when((pl.program_id(0) == i) & (pl.program_id(1) == 0))
        def _(turned_ref=turned_ref):
            x = turned_ref[:width, :].astype(F32)
            start[...] = jnp.concatenate([x[g * per : (g + 1) * per] for g in order], axis=0).astype(BF)

    grad = dot(weight_ref[0], start[...], 1, 0)
    gate = gate_ref[...].astype(F32)
    for c in range(cot_ref.shape[0]):
        lines = slice(c * PIX, (c + 1) * PIX)
        out_ref[0, lines, :] = (grad[lines, :] + gate * cot_ref[c].astype(F32)).astype(BF)


def fields_back(frames, chunk, weight, got, gates, cot, after):
    channels, pixels, patches = cot.shape
    rows = got[0].shape[1]
    width = weight.shape[2]
    return call(
        partial(fields_back_kernel, frames),
        "fields_back",
        shape(EXP, channels * PIX, patches),
        [
            pl.BlockSpec((1, channels * PIX, width), lambda i, e, r: (e, 0, 0)),
            whole(got[0]),
            whole(got[1]),
            pl.BlockSpec((PIX, rows), lambda i, e, r: (e, r[0] ^ i)),
            pl.BlockSpec((channels, PIX, rows), lambda i, e, r: (0, 0, r[0] ^ i)),
        ],
        pl.BlockSpec((1, channels * PIX, rows), lambda i, e, r: (e, 0, r[0] ^ i)),
        grid=(2, EXP),
        scratch=[pltpu.VMEM((width, rows), BF)],
        scalars=1,
        after=after,
    )(chunk, weight, *got, gates, cot)


def norm_parts(v):
    centred = v - jnp.mean(v, axis=-1, keepdims=True)
    spread = jnp.mean(centred * centred, axis=-1, keepdims=True)
    r = lax.rsqrt(spread + epsilon)
    return centred * r, r


def norm_back(grad, n, r, gain):
    t = grad * gain
    return r * (
        t - jnp.mean(t, axis=-1, keepdims=True) - n * jnp.mean(t * n, axis=-1, keepdims=True)
    )


def add_low(a, b):
    return (a.astype(F32) + b.astype(F32)).astype(BF)


def halve(x, axis, mine):
    keep = lax.dynamic_index_in_dim(x, mine, axis, keepdims=False)
    send = lax.dynamic_index_in_dim(x, 1 - mine, axis, keepdims=False)
    return keep, send


def merge_kernel(blocks, side_ref, *refs):
    ins, (send_ref, keep_ref) = refs[:-2], refs[-2:]

    def put(gone, gone_far, kept, kept_far):
        for a, b, out_ref in ((gone, gone_far, send_ref), (kept, kept_far, keep_ref)):
            x = a[...].astype(F32) + b[...].astype(F32)
            out_ref[...] = x.astype(BF).reshape(out_ref.shape)

    if blocks == 0:
        (gone, kept), n = ins[:2], len(ins) // 2 - 1
        for i in range(n):
            far = ins[2 + i], ins[2 + n + i]
            pl.when(pl.program_id(0) == i)(lambda far=far: put(gone, far[0], kept, far[1]))
    elif len(ins) == 4:
        put(*ins)
    else:
        pl.when(pl.program_id(0) < blocks)(lambda: put(*ins[:4]))
        pl.when(pl.program_id(0) == blocks)(lambda: put(*ins[4:]))


def merge(keep, far, side, window, more, cost, after):
    a, _, rows, n = keep.shape
    first, count = window or (0, n)
    if isinstance(far, list):
        return merge_parts(keep, far, side, after)
    block = more[0].shape[3] if more else max(
        b for b in (1024, 768, 640, 384, 256, 128) if count % b == 0 and first % b == 0 and (b < count or b < 512)
    )
    blocks = count // block
    specs = [
        pl.BlockSpec(
            (a, 1, rows, block),
            lambda i, c, flip=flip: (0, c[0] ^ flip, 0, jnp.minimum(i, blocks - 1) + first // block),
        )
        for flip in (1, 1, 0, 0)
    ]
    operands = [keep, far, keep, far]
    if more:
        specs += [
            pl.BlockSpec((a, 1, rows, block), lambda i, c, flip=flip: (0, c[0] ^ flip, 0, 0))
            for flip in (1, 1, 0, 0)
        ]
        operands += [*more, *more]
    steps = blocks + (1 if more else 0)
    out = pl.BlockSpec((a, rows, block), lambda i, c: (0, 0, i))
    return call(
        partial(merge_kernel, blocks),
        "merge",
        [shape(a, rows, steps * block)] * 2,
        specs,
        [out, out],
        grid=(steps,),
        scalars=1,
        cost=cost,
        after=after,
    )(side.astype(jnp.int32)[None], *operands)


def merge_parts(keep, far, side, after):
    a, _, rows, n = keep.shape
    block = n // len(far)

    def spec(flip, step):
        return pl.BlockSpec((a, 1, rows, block), lambda i, c: (0, c[0] ^ flip, 0, i * step))

    out = pl.BlockSpec((a, rows, block), lambda i, c: (0, 0, i))
    return call(
        partial(merge_kernel, 0),
        "merge",
        [shape(a, rows, n)] * 2,
        [spec(1, 1), spec(0, 1), *[spec(1, 0) for _ in far], *[spec(0, 0) for _ in far]],
        [out, out],
        grid=(len(far),),
        scalars=1,
        after=after,
    )(side.astype(jnp.int32)[None], keep, keep, *far, *far)


class Sum:
    def __init__(self, plan, f, z, order, keep, far, window=None, more=None):
        self.plan, self.at, self.order = plan, {"f": f, "z": z}, list(order)
        self.left = sorted(order, key=lambda b: (b[0] != "f", -b[1]))
        self.keep, self.far, self.window, self.more = keep, far, window, more

    def step(self, after, cost=0):
        axis, bit = self.order.pop(0)
        a = 2 ** self.left.index((axis, bit))
        def rows(x):
            return [rows(y) for y in x] if isinstance(x, list) else x.reshape(a, 2, -1, x.shape[-1])

        keep, far, *more = (rows(x) for x in (self.keep, self.far, *(self.more or ())))
        side = (self.at[axis] // bit) % 2
        send, self.keep = merge(keep, far, side, self.window, more, cost, after)
        self.far = (self.plan.swap_frame if axis == "f" else self.plan.swap_chan)(send, bit)
        self.window = self.more = None
        self.left.remove((axis, bit))
        return send

    def finish(self):
        while self.order:
            self.step([])
        n = self.keep.shape[-1]
        return self.keep.reshape(-1, n).astype(F32) + self.far.reshape(-1, n).astype(F32)


def on_device(
    plan,
    fields,
    lead_index,
    embed_weight,
    position_embed,
    lead_table,
    attend_gain,
    attend_shift,
    attend_weight,
    out_weight,
    out_bias,
    mixer_gain,
    mixer_shift,
    up_weight,
    up_bias,
    down_weight,
    down_bias,
    head_weight,
    specialist_cell_offset,
    cotangent,
):
    f, z = lax.axis_index("frames"), lax.axis_index("chan")
    chan, frames = plan.chan, plan.frames
    width = attend_gain.shape[0]
    hidden_width = up_bias.shape[0]
    channels, pixels, patches = cotangent.shape[1:]
    rows = position_embed.shape[0]
    lines = EXP * channels * PIX
    own_fields, cot = fields[0], cotangent[0]
    flat_fields = own_fields.reshape(lines, patches)
    flat_weight = embed_weight.reshape(lines, width)
    offset = specialist_cell_offset[..., None]
    numbers = jnp.stack([z ^ s for s in range(chan)]).astype(jnp.int32)
    mine = (f % 2).astype(jnp.int32)[None]

    onehot = (
        lead_index[:, None] == jnp.arange(lead_table.shape[0], dtype=jnp.int32)[None, :]
    ).astype(BF)
    lead_vector = dot(onehot, lead_table, 1, 0)
    got = []
    for s in reversed(range(chan)):
        block = lax.dynamic_slice(flat_fields, (0, (z ^ s) * rows), (lines, rows))
        part = dot(block, flat_weight, 0, 0)
        if s == 0:
            part = part + position_embed.astype(F32) + lead_vector
        got.append(plan.to_worker(part.astype(BF), s))

    def flag(x):
        return x.astype(jnp.int32)[None]

    core, low = f % 2, z % 2

    pulls = pull(numbers, own_fields, cot, offset)
    vectors = jnp.concatenate([out_bias, mixer_gain, mixer_shift, down_bias, up_bias])[None]

    (head,) = relay([head_weight], [pulls[0]])
    stream_start, normed = first_norm(got, attend_gain, attend_shift, [head, vectors])
    normed_chan = plan.swap_chan(normed, 1)
    near, near_turned, queries = project(normed, plan.swap_frame(normed, 1), attend_weight, True, [])
    pulls = [plan.to_worker(a, s) for s, a in enumerate(pulls)]
    (normed_chan,) = relay([normed_chan], [near])
    far, far_turned = project(normed_chan, plan.swap_frame(normed_chan, 1), attend_weight, False, [])
    attended, attended_turned, shares, rinv = attend(queries, near, far)

    (
        gate, _, mid_grad, attended_low, normed_turned, end_turned, down_low, logit_low, branch_low,
        active_turned, hidden_low,
    ) = middle(stream_start, attended, out_weight, vectors, head, pulls, up_weight, down_weight)

    gate = plan.from_workers(beside(flag(core), gate, plan.swap_frame(gate, 1), []))

    query_low, keep_grad, send_grad = attend_back(queries, near, far, attended, attended_low, shares, rinv, [])
    send = project_back(send_grad, attend_weight, gate)
    keep = project_back(keep_grad, attend_weight, [send], query_low)
    send = plan.swap_frame(send, 1)
    far_grad = (keep[rows:] + send[rows:].astype(F32)).astype(BF)
    going = [far_grad]
    far_grad = plan.swap_chan(far_grad, 1)

    n_wide = hidden_width + (-hidden_width % WIDE) + WIDE
    weights = tall_grads(frames, chan, active_turned, down_low, n_wide, going)
    weights = wide_grads(normed_turned, hidden_low, attended_turned, branch_low, end_turned, logit_low, weights)
    step = weights
    weights = lax.psum_scatter(weights, "frames", scatter_dimension=0, tiled=True)

    sent = start_back(frames, keep, send, far_grad, stream_start, attend_gain, mid_grad, [step])
    sent = beside(flag(core), sent, plan.swap_frame(sent, 1), [])
    got = plan.from_workers(sent)

    *attend_send, attend_keep = attend_grads(
        frames, mine, near_turned, far_turned, query_low, keep_grad, send_grad, [sent]
    )
    high = [("f", bit) for bit in bits_of(frames)[1:]]
    lower = [("z", bit) for bit in bits_of(chan)]
    projections = Sum(plan, f, z, high + lower, attend_keep, [plan.swap_frame(a, 1) for a in attend_send])

    mixed, expert_bias, gates = blend(flag(low), gate, own_fields, cot, offset, attend_send)

    step = projections.step([mixed])
    sides = jnp.concatenate([mine, flag(low), flag(z // plan.half)])
    embed_send, embed_keep, own_send, own_keep, lead = embed_back(sides, got, flat_fields, rows, [step])
    embed_far, own_far = plan.swap_frame(embed_send, 1), plan.swap_frame(own_send, 1)
    cut = (lines // rows + 1) // 2 * rows
    embed_sums = [
        Sum(plan, f, z, high, embed_keep, embed_far, (0, cut)),
        Sum(plan, f, z, high[::-1], embed_keep, embed_far, (cut, lines - cut), (own_keep, own_far)),
    ]
    step = projections.step([embed_send], 30)
    step = embed_sums[0].step([step])
    step = embed_sums[1].step([step])
    (weights,) = relay([weights], [step])
    step = weights
    weights = lax.psum_scatter(weights, "chan", scatter_dimension=0, tiled=True)
    wide_weight = embed_weight.reshape(EXP, channels * PIX, width)

    per = width // frames
    lead = lead[0].reshape(2, frames // 2, per)
    lead = jnp.swapaxes(jnp.where(core == 0, lead[::-1], lead), 0, 1).reshape(-1, rows)
    own = (jnp.arange(frames) == f).astype(F32)
    n_lead = lead.shape[0]
    parts = [
        sum(a[EXP * PIX :, i : i + rows].astype(F32) for a in gate for i in (0, rows)),
        sum(a[width : width + 2 * n_lead, i : i + rows].astype(F32) for a in got for i in (0, rows)),
        (own[:, None, None] * lead).reshape(-1, rows),
        jnp.pad(own * lead_index.astype(F32), (0, rows - frames))[None],
        expert_bias.reshape(-1, rows),
    ]
    small = jnp.concatenate(parts, axis=0)
    (small,) = relay([jnp.pad(small, ((0, -small.shape[0] % 16), (0, 0))).astype(BF)], [step])
    others = iter(bits_of(frames))
    small_far = plan.swap_frame(small, next(others))
    fields_grad = fields_back(frames, flag(low), wide_weight, got, gates, cot, [small])
    step = projections.step([fields_grad])
    step = embed_sums[0].step([step]) if embed_sums[0].order else step
    step = embed_sums[1].step([step, weights]) if embed_sums[1].order else step
    step = projections.step([step])
    for i, bit in enumerate(others):
        small = plus(small, small_far, [step])
        small_far = plan.swap_frame(small, bit)
        step = small

    weights = weights.astype(F32)
    small = small.astype(F32) + small_far.astype(F32)
    cuts, first = [], 0
    for a in parts:
        cuts.append(small[first : first + a.shape[0]])
        first += a.shape[0]
    vectors, norms, lead, index, bias = cuts
    here = f * chan + z
    n_each = width // (frames * chan)

    def own_part(x, n=n_each, axis=0):
        return lax.dynamic_slice_in_dim(x, here * n, n, axis)

    vectors_out = jnp.concatenate([vectors[: 4 * n_lead], norms], axis=0).reshape(6, width)
    vectors_out = own_part(vectors_out, axis=1)
    up_bias_out = own_part(vectors[4 * n_lead :].reshape(-1), hidden_width // (frames * chan))
    rows_of_table = index[0, :frames, None] == jnp.arange(lead_table.shape[0], dtype=F32)[None]
    lead = own_part(lead.reshape(frames, width), axis=1)
    table_out = jnp.sum(rows_of_table[:, :, None].astype(F32) * lead[:, None, :], axis=0)
    bias = lax.dynamic_slice_in_dim(bias.reshape(channels, EXP, PIX), f * (PIX // frames), PIX // frames, 2)
    bias_out = jnp.swapaxes(bias, 0, 1)
    first, second = (a.finish() for a in embed_sums)
    n = lines - first.shape[1]
    embed_out = jnp.concatenate([first, second[:, :n]], axis=1).T.reshape(EXP, channels, PIX, per)
    position_out = second[:, n:].T
    attend_out = projections.finish()
    tall = weights[:, :hidden_width].reshape(n_each, -1, width)
    tall = jnp.swapaxes(tall, 0, 1).reshape(-1, width)
    wide = weights[:, hidden_width:]

    return (
        mixed[None],
        fields_grad.reshape(fields.shape),
        embed_out,
        position_out,
        table_out,
        vectors_out[4],
        vectors_out[5],
        attend_out,
        wide[:, hidden_width : hidden_width + width],
        vectors_out[2],
        vectors_out[0],
        vectors_out[1],
        wide[:, :hidden_width],
        up_bias_out,
        tall,
        vectors_out[3],
        wide[:, hidden_width + width : hidden_width + width + EXP * PIX],
        bias_out,
    )


def solution(mesh):
    plan = Plan(mesh.shape["frames"], mesh.shape["chan"])
    both = ("frames", "chan")
    in_specs = (
        P("frames", None, "chan", None, None),
        P("frames"),
        P(None, "chan", None, None),
        P("chan", None),
        *[P()] * 13,
        P(None, "chan", None),
        P("frames", "chan", None, None),
    )
    out_specs = (
        P("frames", "chan", None, None),
        P("frames", None, "chan", None, None),
        P(None, "chan", None, "frames"),
        P("chan", "frames"),
        P(None, both),
        P(both),
        P(both),
        P(both, None),
        P(both, None),
        P(both),
        P(both),
        P(both),
        P(both, None),
        P(both),
        P(both, None),
        P(both),
        P(both, None),
        P(None, "chan", "frames"),
    )
    return jax.shard_map(
        partial(on_device, plan), mesh=mesh, in_specs=in_specs, out_specs=out_specs, check_vma=False
    )
```
